512 devices in a mesh: cube: 32 (over y_hi, z, core), sub: 16 (over y_lo, x).
Axes of the slice: x: 4, y: 8 (y_hi: 2, y_lo: 4; y = y_hi * 4 + y_lo), z: 8, core: 2. Of those that a mesh axis runs over, the one named last changes fastest.
Arguments:
- leaf_update: float32 [32, 4096, 4096], P('cube', 'sub'), may hold values from -12 to 16, as said below
- maps_low: int32 [32, 32], replicated, may hold values from 0 to 31, as said below
- maps_high: int32 [16, 32], replicated, may hold values from 0 to 31, as said below
Outputs:
- factor_low: float32 [32, 4096, 128], P('cube', 'sub')
- factor_high: float32 [32, 4096, 64], P('cube', 'sub')
The draws below stay inside these ranges and needn't reach their ends.
Inputs may be any that keep to these rules, and one draw needn't show every extreme that they name: `leaf_update`: each of the 32 slices is symmetric positive definite. `maps_low`: each row is a permutation of the 32 tiles that keeps every tile inside its block of 2 consecutive tiles and keeps in place the tiles below 2 and those from 2 to 3. `maps_high`: each row is a permutation of the 32 tiles that keeps every tile inside its block of 2 consecutive tiles and keeps in place the tiles below 2 and those from 2 to 3.
All inputs are finite; a program needn't handle non-finite values.
Results may differ from the reference program's by a relative error of at most 0.0003.
Values sent between devices are 32-bit elements; how exact they have to be, the bound alone decides.
A program may use at most 64 MiB of HBM per device.

```python
import jax
import jax.numpy as jnp
from jax import lax

F = 4096
TILE = 128
PW = 128
PANELS = 2
LEAVES = 32
NT = 32
SEP = 256
ROWS_DEV = 256
BLOCK_TILES = 2


def tile_permutations(key, map_count):
    tile_ids = jnp.arange(NT, dtype=jnp.int32)
    sep_tiles = SEP // TILE
    fixed_mask = (tile_ids < sep_tiles) | (tile_ids >= BLOCK_TILES) & (tile_ids < BLOCK_TILES + sep_tiles)

    def draw_one(subkey):
        shuffled = jax.random.permutation(subkey, NT).astype(jnp.int32)
        scores = tile_ids // BLOCK_TILES * (4 * NT) + jnp.where(fixed_mask, tile_ids, NT + shuffled)
        ordering = jnp.argsort(scores).astype(jnp.int32)
        return jnp.argsort(ordering).astype(jnp.int32)
    return jax.vmap(draw_one)(jax.random.split(key, map_count))


def draw_maps_low(key, part):
    key = jax.random.fold_in(key, 11)
    return tile_permutations(key, LEAVES)


def draw_maps_high(key, part):
    key = jax.random.fold_in(key, 12)
    return tile_permutations(key, LEAVES // 2)


def draw_leaf_update(key, part):
    key = jax.random.fold_in(key, 21)
    inner_rank = F // 4

    def draw_one(subkey):
        key_factor, key_diagonal = jax.random.split(subkey, 2)
        factor = jax.random.truncated_normal(key_factor, -3.0, 3.0, (F, inner_rank), jnp.float32)
        product = jnp.dot(factor, factor.T, precision=lax.Precision.HIGHEST) / inner_rank
        product = 0.5 * (product + product.T)
        diagonal = jax.random.uniform(key_diagonal, (F,), jnp.float32, 0.4, 1.0)
        row_ids = jnp.arange(F, dtype=jnp.int32)[:, None]
        column_ids = jnp.arange(F, dtype=jnp.int32)[None, :]
        matrix = product + jnp.where(row_ids == column_ids, diagonal[:, None], 0.0)
        return matrix
    return lax.map(draw_one, jax.random.split(key, LEAVES))


def setup_inputs(seed: int = 0) -> dict:
    arg_keys = jax.random.split(jax.random.key(seed), 4)
    return {
        "leaf_update": draw_leaf_update(jax.random.fold_in(arg_keys[3], 71), 0),
        "maps_low": draw_maps_low(jax.random.fold_in(arg_keys[3], 71), 0),
        "maps_high": draw_maps_high(jax.random.fold_in(arg_keys[3], 71), 0),
    }


HIGHEST = lax.Precision.HIGHEST

def spread(child_front, tile_map):
    inverse = jnp.argsort(tile_map).astype(jnp.int32)
    source = (inverse[:, None] * TILE + jnp.arange(TILE, dtype=jnp.int32)[None, :]).reshape(-1)
    return jnp.take(jnp.take(child_front, source, axis=0), source, axis=1)

def eliminate(assembled, first_row, is_last):
    lower_factor = jnp.linalg.cholesky(assembled[first_row:first_row + PW, first_row:first_row + PW])
    factor = jax.scipy.linalg.solve_triangular(lower_factor, assembled[:, first_row:first_row + PW].T, lower=True).T
    if is_last:
        return (assembled, factor)
    assembled = assembled - jnp.dot(factor, factor.T, precision=HIGHEST)
    positions = jnp.arange(F, dtype=jnp.int32)
    keep_mask = (positions < first_row) | (positions >= first_row + PW)
    return (jnp.where(keep_mask[:, None] & keep_mask[None, :], assembled, 0.0), factor)

def parent_level(children, tile_maps, tree_level, is_last):
    child_pairs = children.reshape(-1, 2, F, F)
    map_pairs = tile_maps.reshape(-1, 2, tile_maps.shape[1])
    base_row = ROWS_DEV if tree_level == 0 else 0

    def assemble_one(bundle):
        pair_fronts, pair_maps = bundle
        assembled = spread(pair_fronts[0], pair_maps[0]) + spread(pair_fronts[1], pair_maps[1])
        factors = []
        for panel_step in range(PANELS):
            first_row = base_row + panel_step * PW
            assembled, factor = eliminate(assembled, first_row, is_last and panel_step == PANELS - 1)
            factors.append(factor)
        return (assembled, jnp.concatenate(factors, axis=1))
    return lax.map(assemble_one, (child_pairs, map_pairs))

def reference(leaf_update, maps_low, maps_high):
    child_next, panel_first = parent_level(leaf_update, maps_low, 0, False)
    unused, panel_second = parent_level(child_next, maps_high, 1, True)
    lower_part = panel_first.reshape(-1, F, 2, SEP // 2).transpose(0, 2, 1, 3).reshape(-1, F, SEP // 2)
    upper_part = panel_second.reshape(-1, F, 4, SEP // 4).transpose(0, 2, 1, 3).reshape(-1, F, SEP // 4)
    return (lower_part, upper_part)
```

```python
import jax
import jax.numpy as jnp
from jax import lax
from jax.experimental import pallas as pl
from jax.experimental.pallas import tpu as pltpu
from jax.sharding import PartitionSpec as P

SEP = 256
HALF = 128
GROUP = 32
HIGHEST = lax.Precision.HIGHEST
MESH = pl.DeviceIdType.MESH


def dot(a, b):
    return jnp.dot(a, b, precision=HIGHEST, preferred_element_type=jnp.float32)


def dot_nt(a, b):
    return lax.dot_general(
        a, b, (((1,), (1,)), ((), ())), precision=HIGHEST, preferred_element_type=jnp.float32
    )


def lane(x, c):
    return jnp.broadcast_to(x[:, c : c + 1], (x.shape[0], HALF))


def row(x, j):
    return jnp.broadcast_to(x[j : j + 1, :], (8, HALF))


def scaled(x, r):
    n = x.shape[0]
    return (x.reshape(n // 8, 8, HALF) * r[None]).reshape(n, HALF)


def inverse_factor(trail):
    n = trail.shape[0]
    steps = n // 8
    sublane = lax.broadcasted_iota(jnp.int32, (8, HALF), 0)
    unit = (
        lax.broadcasted_iota(jnp.int32, (n, n), 0) == lax.broadcasted_iota(jnp.int32, (n, n), 1)
    ).astype(jnp.float32)
    done = []
    head = [lane(trail[:8], j) for j in range(8)]
    for k in range(steps):
        c0 = 8 * k
        t_head, t_tail = trail[:8], trail[8:]
        u_head, u_tail = unit[:8], unit[8:]
        last = k == steps - 1
        if not last:
            tail = [lane(t_tail, c0 + j) for j in range(8)]
            ahead = [lane(t_tail[:8], c0 + 8 + j) for j in range(8)]
        pivots = None
        for j in range(8):
            pivot = row(head[j], j)
            inv = 1.0 / pivot
            for q in range(j + 1, 8):
                m = row(head[q], j) * inv
                head[q] = head[q] - head[j] * m
                if not last:
                    tail[q] = tail[q] - scaled(tail[j], m)
            below = jnp.where(sublane > j, head[j], 0.0)
            u_row = row(u_head, j) * inv
            u_head = u_head - below * u_row
            if not last:
                first = tail[j][:8]
                for q in range(8):
                    ahead[q] = ahead[q] - first * (row(first, q) * inv)
                t_row = row(t_head, j) * inv
                t_head = t_head - below * t_row
                t_tail = t_tail - scaled(tail[j], t_row)
                u_tail = u_tail - scaled(tail[j], u_row)
            pivots = pivot if pivots is None else jnp.where(sublane == j, pivot, pivots)
        done.append(u_head * lax.rsqrt(pivots))
        if not last:
            trail, unit, head = t_tail, u_tail, ahead
    return jnp.concatenate(done, axis=0)


def inverse_factor_two(block, out_ref):
    inv1 = inverse_factor(block(0, 0))
    low = dot_nt(block(1, 0), inv1)
    inv2 = inverse_factor(block(1, 1) - dot_nt(low, low))
    out_ref[:HALF, :HALF] = inv1
    out_ref[:HALF, HALF:] = jnp.zeros((HALF, HALF), jnp.float32)
    out_ref[HALF:, :HALF] = -dot(inv2, dot(low, inv1))
    out_ref[HALF:, HALF:] = inv2


def kernel(
    maps_low, maps_high, leaf, out_low, out_high,
    slab, slab_in, p_stage, x_stage, pivot, lead, inv, root, panel, schur, schur_in, child, child_in, inv_high,
    load_sem, pair_sems, p_send, p_recv, x_send, x_recv, ps_send, ps_recv, xs_send, xs_recv, z_sems,
):
    cube = lax.axis_index("cube")
    sub = lax.axis_index("sub")
    front = cube // 2
    core = cube % 2
    me = 2 * sub + core

    def peer(i):
        return (2 * front + i % 2, i // 2)

    def rows(i):
        return pl.ds(pl.multiple_of(8 * i, 8), 8)

    partner = (cube + 1 - 2 * core, sub)
    other_front = front + 1 - 2 * (front % 2)
    across = (2 * other_front + core, sub)

    load = pltpu.make_async_copy(leaf.at[0, :, pl.ds(0, 2 * SEP)], slab, load_sem)
    load.start()

    barrier = pltpu.get_barrier_semaphore()

    def greet(t, carry):
        pl.semaphore_signal(barrier, inc=1, device_id=peer((me + t) % GROUP), device_id_type=MESH)
        return carry

    lax.fori_loop(1, GROUP, greet, 0)
    pl.semaphore_signal(barrier, inc=1, device_id=across, device_id_type=MESH)
    pl.semaphore_wait(barrier, GROUP)
    load.wait()

    def p_piece(i):
        return pltpu.make_async_remote_copy(
            src_ref=slab.at[rows(i), pl.ds(SEP, SEP)], dst_ref=p_stage.at[core],
            send_sem=ps_send.at[i], recv_sem=ps_recv.at[core], device_id=peer(i), device_id_type=MESH)

    def x_piece(i):
        return pltpu.make_async_remote_copy(
            src_ref=slab.at[rows(i)], dst_ref=x_stage.at[core],
            send_sem=xs_send.at[i], recv_sem=xs_recv.at[core], device_id=peer(i), device_id_type=MESH)

    def each_peer(fn):
        def step(t, carry):
            fn((me + t) % GROUP)
            return carry

        lax.fori_loop(1, GROUP, step, 0)

    @pl.when(sub == 1)
    def _():
        each_peer(lambda i: p_piece(i).start())
        p_stage[core] = slab[rows(me), SEP:]

    @pl.when(sub == 0)
    def _():
        each_peer(lambda i: x_piece(i).start())
        x_stage[core] = slab[rows(me), :]

    def p_share(i, at):
        return pltpu.make_async_remote_copy(
            src_ref=pivot.at[rows(at)], dst_ref=pivot.at[rows(at)],
            send_sem=p_send.at[i], recv_sem=p_recv.at[at], device_id=peer(i), device_id_type=MESH)

    def x_share(i, at):
        return pltpu.make_async_remote_copy(
            src_ref=lead.at[rows(at)], dst_ref=lead.at[rows(at)],
            send_sem=x_send.at[i], recv_sem=x_recv.at[at], device_id=peer(i), device_id_type=MESH)

    def stage_wait(stage, sems, root_sub):
        for c in range(2):
            @pl.when(jnp.logical_or(sub != root_sub, core != c))
            def _():
                pltpu.make_async_remote_copy(
                    src_ref=stage.at[c], dst_ref=stage.at[c], send_sem=load_sem, recv_sem=sems.at[c],
                    device_id=peer(2 * root_sub + c), device_id_type=MESH).wait_recv()

    stage_wait(p_stage, ps_recv, 1)
    pivot[rows(me), :] = p_stage[0] + p_stage[1]
    each_peer(lambda i: p_share(i, me).start())
    stage_wait(x_stage, xs_recv, 0)
    lead[rows(me), :] = x_stage[0] + x_stage[1]
    each_peer(lambda i: x_share(i, me).start())
    pair = pltpu.make_async_remote_copy(
        src_ref=slab, dst_ref=slab_in, send_sem=pair_sems.at[0], recv_sem=pair_sems.at[1],
        device_id=partner, device_id_type=MESH)
    pair.start()

    each_peer(lambda i: p_share(i, i).wait_recv())

    def pivot_quarter(i, j):
        return pivot[i * HALF : (i + 1) * HALF, j * HALF : (j + 1) * HALF]

    inverse_factor_two(pivot_quarter, inv)
    each_peer(lambda i: x_share(i, i).wait_recv())
    root[...] = dot_nt(lead[:, SEP:], inv[...])
    schur[...] = lead[:, :SEP] - dot_nt(root[...], root[...])
    z_schur = pltpu.make_async_remote_copy(
        src_ref=schur, dst_ref=schur_in, send_sem=z_sems.at[0], recv_sem=z_sems.at[1],
        device_id=across, device_id_type=MESH)
    z_schur.start()

    pair.wait_recv()

    def tiles(ref, table, index):
        moved = jnp.full((HALF, ref.shape[1]), table[index, 2 * sub], jnp.int32) != 2 * sub
        first, second = ref[:HALF, :], ref[HALF:, :]
        return jnp.where(moved, second, first), jnp.where(moved, first, second)

    own = tiles(slab, maps_low, cube)
    theirs = tiles(slab_in, maps_low, cube + 1 - 2 * core)
    keep = (sub != 1).astype(jnp.float32)
    for half in range(2):
        both = own[half] + theirs[half]
        w = dot_nt(both[:, SEP:], inv[...])
        at = slice(half * HALF, (half + 1) * HALF)
        panel[0, at, :] = w[:, :HALF]
        panel[1, at, :] = w[:, HALF:]
        child[at, :] = (both[:, :SEP] - dot_nt(w, root[...])) * keep
    z_child = pltpu.make_async_remote_copy(
        src_ref=child, dst_ref=child_in, send_sem=z_sems.at[2], recv_sem=z_sems.at[3],
        device_id=across, device_id_type=MESH)
    z_child.start()
    out_low[0] = panel[core]

    z_schur.wait_recv()

    def schur_quarter(i, j):
        at = (slice(i * HALF, (i + 1) * HALF), slice(j * HALF, (j + 1) * HALF))
        return schur[at] + schur_in[at]

    inverse_factor_two(schur_quarter, inv_high)
    z_child.wait_recv()
    own = tiles(child, maps_high, front)
    theirs = tiles(child_in, maps_high, other_front)
    share = inv_high[pl.ds(pl.multiple_of(cube % 4 * 64, 64), 64), :]
    for half in range(2):
        out_high[0, half * HALF : (half + 1) * HALF, :] = dot_nt(own[half] + theirs[half], share)

    z_schur.wait_send()
    z_child.wait_send()
    pair.wait_send()
    each_peer(lambda i: p_share(i, me).wait_send())
    each_peer(lambda i: x_share(i, me).wait_send())

    @pl.when(sub == 1)
    def _():
        each_peer(lambda i: p_piece(i).wait_send())

    @pl.when(sub == 0)
    def _():
        each_peer(lambda i: x_piece(i).wait_send())


def body(leaf_update, maps_low, maps_high):
    f32 = jnp.float32
    dma = pltpu.SemaphoreType.DMA
    return pl.pallas_call(
        kernel,
        out_shape=(
            jax.ShapeDtypeStruct((1, SEP, HALF), f32),
            jax.ShapeDtypeStruct((1, SEP, HALF // 2), f32),
        ),
        in_specs=[
            pl.BlockSpec(memory_space=pltpu.SMEM),
            pl.BlockSpec(memory_space=pltpu.SMEM),
            pl.BlockSpec(memory_space=pl.ANY),
        ],
        out_specs=(pl.BlockSpec(memory_space=pltpu.VMEM), pl.BlockSpec(memory_space=pltpu.VMEM)),
        scratch_shapes=[
            pltpu.VMEM((SEP, 2 * SEP), f32), pltpu.VMEM((SEP, 2 * SEP), f32),
            pltpu.VMEM((2, 8, SEP), f32), pltpu.VMEM((2, 8, 2 * SEP), f32),
            pltpu.VMEM((SEP, SEP), f32), pltpu.VMEM((SEP, 2 * SEP), f32),
            pltpu.VMEM((SEP, SEP), f32), pltpu.VMEM((SEP, SEP), f32), pltpu.VMEM((2, SEP, HALF), f32),
            pltpu.VMEM((SEP, SEP), f32), pltpu.VMEM((SEP, SEP), f32),
            pltpu.VMEM((SEP, SEP), f32), pltpu.VMEM((SEP, SEP), f32), pltpu.VMEM((SEP, SEP), f32),
            dma, dma((2,)), dma((GROUP,)), dma((GROUP,)), dma((GROUP,)), dma((GROUP,)),
            dma((GROUP,)), dma((2,)), dma((GROUP,)), dma((2,)), dma((4,)),
        ],
        compiler_params=pltpu.CompilerParams(
            collective_id=0, has_side_effects=True, vmem_limit_bytes=32 * 1024 * 1024
        ),
        cost_estimate=pl.CostEstimate(flops=2_000_000_000, bytes_accessed=1_000_000, transcendentals=0),
    )(maps_low, maps_high, leaf_update)


def solution(mesh):
    in_specs = (P("cube", "sub", None), P(), P())
    out_specs = (P("cube", "sub", None), P("cube", "sub", None))
    return jax.shard_map(body, mesh=mesh, in_specs=in_specs, out_specs=out_specs, check_vma=False)
```

```python
import jax
import jax.numpy as jnp
from jax import lax
from jax.experimental import pallas as pl
from jax.experimental.pallas import tpu as pltpu
from jax.sharding import PartitionSpec as P

SEP = 256
HALF = 128
BLOCKS = 16
HIGHEST = lax.Precision.HIGHEST
MESH = pl.DeviceIdType.MESH


def dot(a, b):
    return jnp.dot(a, b, precision=HIGHEST, preferred_element_type=jnp.float32)


def dot_nt(a, b):
    return lax.dot_general(
        a, b, (((1,), (1,)), ((), ())), precision=HIGHEST, preferred_element_type=jnp.float32
    )


def lane(x, c):
    return jnp.broadcast_to(x[:, c : c + 1], (x.shape[0], HALF))


def row(x, j):
    return jnp.broadcast_to(x[j : j + 1, :], (8, HALF))


def scaled(x, r):
    n = x.shape[0]
    return (x.reshape(n // 8, 8, HALF) * r[None]).reshape(n, HALF)


def inverse_factor(trail):
    n = trail.shape[0]
    steps = n // 8
    sublane = lax.broadcasted_iota(jnp.int32, (8, HALF), 0)
    unit = (
        lax.broadcasted_iota(jnp.int32, (n, n), 0) == lax.broadcasted_iota(jnp.int32, (n, n), 1)
    ).astype(jnp.float32)
    done = []
    head = [lane(trail[:8], j) for j in range(8)]
    for k in range(steps):
        c0 = 8 * k
        t_head, t_tail = trail[:8], trail[8:]
        u_head, u_tail = unit[:8], unit[8:]
        last = k == steps - 1
        if not last:
            tail = [lane(t_tail, c0 + j) for j in range(8)]
            ahead = [lane(t_tail[:8], c0 + 8 + j) for j in range(8)]
        pivots = None
        for j in range(8):
            pivot = row(head[j], j)
            inv = 1.0 / pivot
            for q in range(j + 1, 8):
                m = row(head[q], j) * inv
                head[q] = head[q] - head[j] * m
                if not last:
                    tail[q] = tail[q] - scaled(tail[j], m)
            below = jnp.where(sublane > j, head[j], 0.0)
            u_row = row(u_head, j) * inv
            u_head = u_head - below * u_row
            if not last:
                first = tail[j][:8]
                for q in range(8):
                    ahead[q] = ahead[q] - first * (row(first, q) * inv)
                t_row = row(t_head, j) * inv
                t_head = t_head - below * t_row
                t_tail = t_tail - scaled(tail[j], t_row)
                u_tail = u_tail - scaled(tail[j], u_row)
            pivots = pivot if pivots is None else jnp.where(sublane == j, pivot, pivots)
        done.append(u_head * lax.rsqrt(pivots))
        if not last:
            trail, unit, head = t_tail, u_tail, ahead
    return jnp.concatenate(done, axis=0)


def inverse_pair(first, second, out_ref):
    inv1 = inverse_factor(first())
    below = second()
    low = dot_nt(below[:, :HALF], inv1)
    inv2 = inverse_factor(below[:, HALF:] - dot_nt(low, low))
    out_ref[:HALF, :HALF] = inv1
    out_ref[:HALF, HALF:] = jnp.zeros((HALF, HALF), jnp.float32)
    out_ref[HALF:, :HALF] = -dot(inv2, dot(low, inv1))
    out_ref[HALF:, HALF:] = inv2


def kernel(
    maps_low, maps_high, leaf, out_low, out_high,
    slab, slab_in, front, p1, p2, lead, inv, root, root_in, panel, c1, c2, child, inv_high,
    low_table, high_table, table_sems, load_sems, pair_sems,
    p1_cut, p1_send, p1_recv, p2_cut, p2_send, p2_recv, lead_cut, lead_send, lead_recv,
    root_sems, c1_send, c1_recv, c2_send, c2_recv, child_send, child_recv,
):
    cube = lax.axis_index("cube")
    sub = lax.axis_index("sub")
    node = cube // 2
    core = cube % 2
    upper = node % 2
    other = node + 1 - 2 * upper
    partner = (cube + 1 - 2 * core, sub)
    across = (2 * other + core, sub)
    diagonal = (2 * other + 1 - core, sub)
    later, sooner = pl.ds(SEP, SEP), pl.ds(0, SEP)

    def remote(src, dst, send_sem, recv_sem, device):
        return pltpu.make_async_remote_copy(
            src_ref=src, dst_ref=dst, send_sem=send_sem, recv_sem=recv_sem, device_id=device, device_id_type=MESH
        )

    def rows(i, base=0):
        return pl.ds(pl.multiple_of(base + 8 * i, 8), 8)

    def each_peer(fn):
        def step(t, carry):
            fn((sub + t) % BLOCKS)
            return carry

        lax.fori_loop(1, BLOCKS, step, 0)

    loads = [
        pltpu.make_async_copy(leaf.at[0, :, cols], slab.at[:, cols], load_sems.at[i])
        for i, cols in enumerate((later, sooner))
    ]
    tables = [
        pltpu.make_async_copy(maps_low, low_table, table_sems.at[0]),
        pltpu.make_async_copy(maps_high, high_table, table_sems.at[1]),
    ]
    for copy in loads + tables:
        copy.start()

    barrier = pltpu.get_barrier_semaphore()

    def greet(device):
        pl.semaphore_signal(barrier, inc=1, device_id=device, device_id_type=MESH)

    for device in (partner, across, diagonal):
        greet(device)
    each_peer(lambda i: greet((cube, i)))
    for copy in tables + loads:
        copy.wait()
    pl.semaphore_wait(barrier, BLOCKS + 2)

    pairs = [
        remote(slab.at[:, cols], slab_in.at[:, cols], pair_sems.at[0, i], pair_sems.at[1, i], partner)
        for i, cols in enumerate((later, sooner))
    ]
    for copy in pairs:
        copy.start()

    def tiles(block, table, index):
        moved = jnp.full((HALF, block.shape[1]), table[index, 2 * sub], jnp.int32) != 2 * sub
        first, second = block[:HALF, :], block[HALF:, :]
        return jnp.where(moved, second, first), jnp.where(moved, first, second)

    def extend_add(cols):
        own = tiles(slab[:, cols], low_table, cube)
        theirs = tiles(slab_in[:, cols], low_table, cube + 1 - 2 * core)
        front[:HALF, cols] = own[0] + theirs[0]
        front[HALF:, cols] = own[1] + theirs[1]

    def p1_piece(i):
        return remote(front.at[rows(i), pl.ds(SEP, HALF)], p1.at[rows(i)], p1_cut.at[i], p1_recv.at[i], (cube, i))

    def p2_piece(i):
        return remote(front.at[rows(i, HALF), later], p2.at[rows(i)], p2_cut.at[i], p2_recv.at[i], (cube, i))

    def lead_piece(i):
        return remote(
            front.at[rows(i, core * HALF)], lead.at[rows(i)], lead_cut.at[i], lead_recv.at[i], (cube, i)
        )

    def share(block, send, recv, at, i):
        return remote(block.at[rows(at)], block.at[rows(at)], send.at[i], recv.at[at], (cube, i))

    def pass_on(block, send, recv, owner):
        @pl.when(sub != owner)
        def _():
            share(block, send, recv, sub, owner).wait_recv()

        each_peer(lambda i: share(block, send, recv, sub, i).start())

    def gathered(block, send, recv):
        each_peer(lambda i: share(block, send, recv, i, i).wait_recv())

    pairs[0].wait_recv()
    extend_add(slice(SEP, 2 * SEP))

    @pl.when(sub == 1)
    def _():
        each_peer(lambda i: p1_piece(i).start())
        each_peer(lambda i: p2_piece(i).start())
        p1[rows(sub), :] = front[rows(sub), SEP : SEP + HALF]
        p2[rows(sub), :] = front[rows(sub, HALF), SEP:]

    pairs[1].wait_recv()
    extend_add(slice(0, SEP))

    @pl.when(sub == 0)
    def _():
        each_peer(lambda i: lead_piece(i).start())
        lead[rows(sub), :] = front[rows(sub, core * HALF), :]

    pass_on(p1, p1_send, p1_recv, 1)
    pass_on(p2, p2_send, p2_recv, 1)
    pass_on(lead, lead_send, lead_recv, 0)

    def p1_block():
        gathered(p1, p1_send, p1_recv)
        return p1[...]

    def p2_block():
        gathered(p2, p2_send, p2_recv)
        return p2[...]

    inverse_pair(p1_block, p2_block, inv)
    gathered(lead, lead_send, lead_recv)
    root[...] = dot_nt(lead[:, SEP:], inv[...])
    root_copy = remote(root, root_in, root_sems.at[0], root_sems.at[1], partner)
    c1_copies = [
        remote(c1.at[0], c1.at[slot], c1_send.at[i], c1_recv.at[slot], device)
        for i, (slot, device) in enumerate(((0, partner), (1, across), (1, diagonal)))
    ]
    c2_copies = [
        remote(c2.at[0], c2.at[slot], c2_send.at[i], c2_recv.at[slot], device)
        for i, (slot, device) in enumerate(((0, partner), (1, across), (1, diagonal)))
    ]

    @pl.when(core == 0)
    def _():
        root_copy.start()
        c1[0] = lead[:, :HALF] - dot_nt(root[...], root[...])
        for copy in c1_copies:
            copy.start()

    @pl.when(core == 1)
    def _():
        c2[0, :, HALF:] = lead[:, HALF:SEP] - dot_nt(root[...], root[...])
        root_copy.wait_recv()
        c2[0, :, :HALF] = lead[:, :HALF] - dot_nt(root[...], root_in[...])
        for copy in c2_copies:
            copy.start()

    keep = (sub != 1).astype(jnp.float32)
    w = dot_nt(front[:, SEP:], inv[...])
    panel[0] = w[:, :HALF]
    panel[1] = w[:, HALF:]
    out_low[0] = panel[core]
    own_columns = front[:, pl.ds(pl.multiple_of(core * HALF, HALF), HALF)]
    child[core] = (own_columns - dot_nt(w, root[...])) * keep
    mine, theirs = child.at[core], child.at[2 + core]
    child_copies = [
        remote(mine, mine, child_send.at[0], child_recv.at[core], partner),
        remote(mine, theirs, child_send.at[1], child_recv.at[2 + core], across),
        remote(mine, theirs, child_send.at[2], child_recv.at[2 + core], diagonal),
    ]
    sent = [jnp.logical_or(core == 0, upper == 1), *[jnp.logical_or(core == 0, upper == 0)] * 2]
    for copy, wanted in zip(child_copies, sent):
        pl.when(wanted)(copy.start)

    def c1_block():
        @pl.when(core == 1)
        def _():
            c1_copies[0].wait_recv()

        c1_copies[1].wait_recv()
        return c1[0] + c1[1]

    def c2_block():
        @pl.when(core == 0)
        def _():
            c2_copies[0].wait_recv()

        c2_copies[1].wait_recv()
        return c2[0] + c2[1]

    inverse_pair(c1_block, c2_block, inv_high)

    def child_wait(slot):
        remote(child.at[slot], child.at[slot], child_send.at[0], child_recv.at[slot], partner).wait_recv()

    def high_columns(half):
        own = tiles(child[half], high_table, node)
        theirs = tiles(child[2 + half], high_table, other)
        return jnp.concatenate([own[0] + theirs[0], own[1] + theirs[1]], axis=0)

    pl.when(core == 1)(lambda: child_wait(0))
    child_wait(2)
    mine = pl.ds(pl.multiple_of(cube % 4 * 64, 64), 64)
    out_high[...] = dot_nt(inv_high[mine, :HALF], high_columns(0))

    @pl.when(upper == 1)
    def _():
        pl.when(core == 0)(lambda: child_wait(1))
        child_wait(3)
        out_high[...] = out_high[...] + dot_nt(inv_high[mine, HALF:], high_columns(1))

    for copy in pairs:
        copy.wait_send()
    for block, send, recv in ((p1, p1_send, p1_recv), (p2, p2_send, p2_recv), (lead, lead_send, lead_recv)):
        each_peer(lambda i: share(block, send, recv, sub, i).wait_send())

    @pl.when(sub == 1)
    def _():
        each_peer(lambda i: p1_piece(i).wait_send())
        each_peer(lambda i: p2_piece(i).wait_send())

    @pl.when(sub == 0)
    def _():
        each_peer(lambda i: lead_piece(i).wait_send())

    @pl.when(core == 0)
    def _():
        root_copy.wait_send()
        for copy in c1_copies:
            copy.wait_send()

    @pl.when(core == 1)
    def _():
        for copy in c2_copies:
            copy.wait_send()

    for copy, wanted in zip(child_copies, sent):
        pl.when(wanted)(copy.wait_send)


def body(leaf_update, maps_low, maps_high):
    dma = pltpu.SemaphoreType.DMA

    def vmem(*shape):
        return pltpu.VMEM(shape, jnp.float32)

    low, high = pl.pallas_call(
        kernel,
        out_shape=(
            jax.ShapeDtypeStruct((1, SEP, HALF), jnp.float32),
            jax.ShapeDtypeStruct((HALF // 2, SEP), jnp.float32),
        ),
        in_specs=[pl.BlockSpec(memory_space=pl.ANY)] * 3,
        out_specs=(pl.BlockSpec(memory_space=pltpu.VMEM), pl.BlockSpec(memory_space=pltpu.VMEM)),
        scratch_shapes=[
            vmem(SEP, 2 * SEP), vmem(SEP, 2 * SEP), vmem(SEP, 2 * SEP),
            vmem(HALF, HALF), vmem(HALF, SEP), vmem(HALF, 2 * SEP),
            vmem(SEP, SEP), vmem(HALF, SEP), vmem(HALF, SEP), vmem(2, SEP, HALF),
            vmem(2, HALF, HALF), vmem(2, HALF, SEP), vmem(4, SEP, HALF), vmem(SEP, SEP),
            pltpu.SMEM((32, 32), jnp.int32), pltpu.SMEM((16, 32), jnp.int32), dma((2,)), dma((2,)), dma((2, 2)),
            *[dma((BLOCKS,))] * 9,
            dma((2,)), dma((3,)), dma((2,)), dma((3,)), dma((2,)), dma((3,)), dma((4,)),
        ],
        compiler_params=pltpu.CompilerParams(
            collective_id=0, has_side_effects=True, vmem_limit_bytes=64 * 1024 * 1024
        ),
        cost_estimate=pl.CostEstimate(flops=2_000_000_000, bytes_accessed=1_000_000, transcendentals=0),
    )(maps_low, maps_high, leaf_update)
    return low, high.T[None]


def solution(mesh):
    in_specs = (P("cube", "sub", None), P(), P())
    out_specs = (P("cube", "sub", None), P("cube", "sub", None))
    return jax.shard_map(body, mesh=mesh, in_specs=in_specs, out_specs=out_specs, check_vma=False)
```

```python
import jax
import jax.numpy as jnp
from jax import lax
from jax.experimental import pallas as pl
from jax.experimental.pallas import tpu as pltpu
from jax.sharding import PartitionSpec as P

SEP = 256
HALF = 128
BLOCKS = 16
BAND = 4
HOOK = 10
HIGHEST = lax.Precision.HIGHEST
MESH = pl.DeviceIdType.MESH


def dot(a, b):
    return jnp.dot(a, b, precision=HIGHEST, preferred_element_type=jnp.float32)


def dot_nt(a, b):
    return lax.dot_general(
        a, b, (((1,), (1,)), ((), ())), precision=HIGHEST, preferred_element_type=jnp.float32
    )


def pieces(x):
    high = x.astype(jnp.bfloat16)
    rest = x - high.astype(jnp.float32)
    mid = rest.astype(jnp.bfloat16)
    return high, mid, (rest - mid.astype(jnp.float32)).astype(jnp.bfloat16)


def stacked(a, b, a_axis, b_axis):
    ah, am, al = pieces(a)
    bh, bm, bl = pieces(b)
    return lax.dot_general(
        jnp.concatenate([ah, ah, am, am, ah, al], axis=a_axis),
        jnp.concatenate([bh, bm, bh, bm, bl, bh], axis=b_axis),
        (((a_axis,), (b_axis,)), ((), ())),
        preferred_element_type=jnp.float32,
    )


def nt(a, b):
    return stacked(a, b, 1, 1)


def lane(x, c):
    return jnp.broadcast_to(x[:, c : c + 1], (x.shape[0], HALF))


def row(x, j):
    return jnp.broadcast_to(x[j : j + 1, :], (8, HALF))


def scaled(x, r):
    n = x.shape[0]
    return (x.reshape(n // 8, 8, HALF) * r[None]).reshape(n, HALF)


def inverse_factor(block, hook_at=None, hook=None):
    n = block.shape[0]
    steps = n // 8
    sublane = lax.broadcasted_iota(jnp.int32, (8, HALF), 0)
    eye = (
        lax.broadcasted_iota(jnp.int32, (n, n), 0) == lax.broadcasted_iota(jnp.int32, (n, n), 1)
    ).astype(jnp.float32)
    near = 8 * (BAND + 1)
    trail, far = block[:near], block[near:]
    unit, far_unit = eye[:near], eye[near:]
    done = []
    head = [lane(trail[:8], j) for j in range(8)]
    for k in range(steps):
        if hook is not None and k == hook_at:
            hook()
        c0 = 8 * k
        t_head, t_tail = trail[:8], trail[8:]
        u_head, u_tail = unit[:8], unit[8:]
        last = k == steps - 1
        if k % BAND == 0:
            band_rows, band_unit = [], []
        if not last:
            tail = [lane(t_tail, c0 + j) for j in range(8)]
            ahead = [lane(t_tail[:8], c0 + 8 + j) for j in range(8)]
        pivots = None
        for j in range(8):
            pivot = row(head[j], j)
            if j % 2 == 0:
                inv = 1.0 / pivot
                beside = row(head[j + 1], j)
                inv_next = pivot * (1.0 / (pivot * row(head[j + 1], j + 1) - beside * beside))
            else:
                inv = inv_next
            head_inv = head[j] * inv
            for q in range(j + 1, 8):
                m = row(head[q], j) * inv if q <= j + 2 else row(head_inv, q)
                head[q] = head[q] - head[j] * m
                if not last:
                    tail[q] = tail[q] - scaled(tail[j], m)
            below = jnp.where(sublane > j, head[j], 0.0)
            u_row = row(u_head, j) * inv
            u_head = u_head - below * u_row
            if not last:
                first = tail[j][:8]
                first_inv = first * inv
                for q in range(8):
                    ahead[q] = ahead[q] - first * row(first_inv, q)
                t_row = row(t_head, j) * inv
                t_head = t_head - below * t_row
                t_tail = t_tail - scaled(tail[j], t_row)
                u_tail = u_tail - scaled(tail[j], u_row)
            pivots = pivot if pivots is None else jnp.where(sublane == j, pivot, pivots)
        scale = lax.rsqrt(pivots)
        done.append(u_head * scale)
        if last:
            break
        band_rows.append(t_head * scale)
        band_unit.append(done[-1])
        trail, unit, head = t_tail, u_tail, ahead
        if k % BAND == BAND - 1 and far is not None:
            top = n - far.shape[0]
            rows_done = jnp.concatenate(band_rows, axis=0)
            ahead_rows = rows_done[:, top:]
            far = far - stacked(ahead_rows, rows_done, 0, 0)
            far_unit = far_unit - stacked(ahead_rows, jnp.concatenate(band_unit, axis=0), 0, 0)
            take = min(8 * BAND, n - top)
            trail = jnp.concatenate([trail, far[:take]], axis=0)
            unit = jnp.concatenate([unit, far_unit[:take]], axis=0)
            far, far_unit = (far[take:], far_unit[take:]) if top + take < n else (None, None)
    return jnp.concatenate(done, axis=0)


def kernel(
    maps_low, maps_high, leaf, out_low, out_high,
    slab, slab_in, front, p1, p2, lead, inv, root, root_in, panel, c1, c2, q2, child, high, inv_high,
    low_table, high_table, table_sems, load_sems, pair_sems,
    p1_cut, p2_cut, lead_cut, gather_send, gather_recv, piece_recv,
    root_sems, c1_send, c1_recv, c2_sems, q2_sems, child_send, child_recv, high_sems,
):
    cube = lax.axis_index("cube")
    sub = lax.axis_index("sub")
    node = cube // 2
    core = cube % 2
    upper = node % 2
    other = node + 1 - 2 * upper
    partner = (cube + 1 - 2 * core, sub)
    across = (2 * other + core, sub)
    diagonal = (2 * other + 1 - core, sub)
    parts = ((SEP, HALF), (SEP + HALF, HALF), (0, SEP))

    def remote(src, dst, send_sem, recv_sem, device):
        return pltpu.make_async_remote_copy(
            src_ref=src, dst_ref=dst, send_sem=send_sem, recv_sem=recv_sem, device_id=device, device_id_type=MESH
        )

    def rows(i, base=0):
        return pl.ds(pl.multiple_of(base + 8 * i, 8), 8)

    def each_peer(fn):
        def step(t, carry):
            fn((sub + t) % BLOCKS)
            return carry

        lax.fori_loop(1, BLOCKS, step, 0)

    loads = [
        pltpu.make_async_copy(leaf.at[0, :, pl.ds(*part)], slab.at[:, pl.ds(*part)], load_sems.at[i])
        for i, part in enumerate(parts)
    ]
    tables = [
        pltpu.make_async_copy(maps_low, low_table, table_sems.at[0]),
        pltpu.make_async_copy(maps_high, high_table, table_sems.at[1]),
    ]
    for copy in loads + tables:
        copy.start()

    barrier = pltpu.get_barrier_semaphore()

    def greet(device):
        pl.semaphore_signal(barrier, inc=1, device_id=device, device_id_type=MESH)

    for device in (partner, across, diagonal):
        greet(device)
    each_peer(lambda i: greet((cube, i)))
    for copy in tables + loads:
        copy.wait()
    pl.semaphore_wait(barrier, BLOCKS + 2)

    pairs = [
        remote(slab.at[:, pl.ds(*part)], slab_in.at[:, pl.ds(*part)], pair_sems.at[0, i], pair_sems.at[1, i], partner)
        for i, part in enumerate(parts)
    ]
    for copy in pairs:
        copy.start()

    def tiles(block, table, index):
        moved = jnp.full((HALF, block.shape[1]), table[index, 2 * sub], jnp.int32) != 2 * sub
        first, second = block[:HALF, :], block[HALF:, :]
        return jnp.where(moved, second, first), jnp.where(moved, first, second)

    def extend_add(i):
        pairs[i].wait_recv()
        cols = slice(parts[i][0], sum(parts[i]))
        own = tiles(slab[:, cols], low_table, cube)
        theirs = tiles(slab_in[:, cols], low_table, cube + 1 - 2 * core)
        front[:HALF, cols] = own[0] + theirs[0]
        front[HALF:, cols] = own[1] + theirs[1]

    def p1_piece(i):
        return remote(front.at[rows(i), pl.ds(SEP, HALF)], p1.at[rows(i)], p1_cut.at[i], piece_recv.at[0], (cube, i))

    def p2_piece(i):
        return remote(front.at[rows(i, HALF), pl.ds(SEP, SEP)], p2.at[rows(i)], p2_cut.at[i], piece_recv.at[1], (cube, i))

    def lead_piece(i):
        return remote(front.at[rows(i, core * HALF)], lead.at[rows(i)], lead_cut.at[i], piece_recv.at[2], (cube, i))

    blocks = (p1, p2, lead)

    def share(n, i):
        own = blocks[n].at[rows(sub)]
        return remote(own, own, gather_send.at[n], gather_recv.at[n], (cube, i))

    def pass_on(n, owner):
        own = blocks[n].at[rows(sub)]

        @pl.when(sub != owner)
        def _():
            remote(own, own, gather_send.at[n], piece_recv.at[n], (cube, owner)).wait_recv()

        each_peer(lambda i: share(n, i).start())

    def all_shares(n):
        others = blocks[n].at[pl.ds(0, 8 * (BLOCKS - 1))]
        return remote(others, others, gather_send.at[n], gather_recv.at[n], partner)

    extend_add(0)

    @pl.when(sub == 1)
    def _():
        each_peer(lambda i: p1_piece(i).start())
        p1[rows(sub), :] = front[rows(sub), SEP : SEP + HALF]

    extend_add(1)

    @pl.when(sub == 1)
    def _():
        each_peer(lambda i: p2_piece(i).start())
        p2[rows(sub), :] = front[rows(sub, HALF), SEP:]

    extend_add(2)

    @pl.when(sub == 0)
    def _():
        each_peer(lambda i: lead_piece(i).start())
        lead[rows(sub), :] = front[rows(sub, core * HALF), :]

    pass_on(0, 1)
    pass_on(1, 1)
    pass_on(2, 0)

    all_shares(0).wait_recv()
    inv1 = inverse_factor(p1[...])
    inv[:HALF, :HALF] = inv1
    inv[:HALF, HALF:] = jnp.zeros((HALF, HALF), jnp.float32)
    all_shares(1).wait_recv()
    low = nt(p2[:, :HALF], inv1)
    inv2 = inverse_factor(p2[:, HALF:] - nt(low, low))
    inv[HALF:, HALF:] = inv2
    all_shares(2).wait_recv()
    root1 = nt(lead[:, SEP : SEP + HALF], inv1)
    root2 = nt(lead[:, SEP + HALF :] - nt(root1, low), inv2)
    root[:, :HALF] = root1
    root[:, HALF:] = root2
    root_copy = remote(root, root_in, root_sems.at[0], root_sems.at[1], partner)
    c1_copies = [
        remote(c1.at[0], c1.at[slot], c1_send.at[i], c1_recv.at[slot], device)
        for i, (slot, device) in enumerate(((0, partner), (1, across), (1, diagonal)))
    ]
    c2_copy = remote(c2.at[0], c2.at[1], c2_sems.at[0], c2_sems.at[1], across)

    @pl.when(core == 0)
    def _():
        c1[0] = lead[:, :HALF] - nt(root1, root1) - nt(root2, root2)
        for copy in reversed(c1_copies):
            copy.start()
        root_copy.start()

    @pl.when(core == 1)
    def _():
        c2[0, :, HALF:] = lead[:, HALF:SEP] - nt(root1, root1) - nt(root2, root2)
        root_copy.wait_recv()
        c2[0, :, :HALF] = lead[:, :HALF] - nt(root1, root_in[:, :HALF]) - nt(root2, root_in[:, HALF:])
        pl.when(upper == 0)(c2_copy.start)

    inv[HALF:, :HALF] = -dot(inv2, dot(low, inv1))
    keep = (sub != 1).astype(jnp.float32)
    w = dot_nt(front[:, SEP:], inv[...])
    own_columns = front[:, pl.ds(pl.multiple_of(core * HALF, HALF), HALF)]
    child[core] = (own_columns - dot_nt(w, root[...])) * keep
    mine, theirs = child.at[core], child.at[2 + core]
    child_copies = [
        (remote(mine, theirs, child_send.at[0], child_recv.at[2 + core], across), jnp.logical_or(core == 0, upper == 0)),
        (remote(mine, mine, child_send.at[1], child_recv.at[core], partner), jnp.logical_and(core == 0, upper == 0)),
        (remote(mine, theirs, child_send.at[2], child_recv.at[2 + core], diagonal), jnp.logical_and(core == 0, upper == 1)),
    ]
    for copy, wanted in child_copies:
        pl.when(wanted)(copy.start)
    panel[0] = w[:, :HALF]
    panel[1] = w[:, HALF:]
    out_low[0] = panel[core]

    pl.when(core == 1)(c1_copies[0].wait_recv)
    c1_copies[1].wait_recv()
    high1 = inverse_factor(c1[0] + c1[1])
    inv_high[...] = high1
    share_rows = pl.ds(pl.multiple_of(core * 64, 64), 64)

    def child_wait(slot):
        remote(child.at[slot], child.at[slot], child_send.at[0], child_recv.at[slot], partner).wait_recv()

    def high_columns(half):
        own = tiles(child[half], high_table, node)
        theirs = tiles(child[2 + half], high_table, other)
        return jnp.concatenate([own[0] + theirs[0], own[1] + theirs[1]], axis=0)

    q2_copy = remote(q2, q2, q2_sems.at[0], q2_sems.at[1], partner)
    high_copy = remote(high.at[core], high.at[core], high_sems.at[0], high_sems.at[1], partner)

    @pl.when(upper == 0)
    def _():
        pl.when(core == 1)(lambda: child_wait(0))
        child_wait(2)
        out_high[...] = nt(inv_high[share_rows, :], high_columns(0))

    @pl.when(upper == 1)
    def _():
        @pl.when(core == 1)
        def _():
            c2_copy.wait_recv()
            q2[...] = c2[0] + c2[1]
            q2_copy.start()

        pl.when(core == 0)(q2_copy.wait_recv)
        high_low = nt(q2[:, :HALF], high1)

        def own_high():
            child_wait(2 + core)
            high[core] = high_columns(core)
            high_copy.start()

        high2 = inverse_factor(q2[:, HALF:] - nt(high_low, high_low), HOOK, own_high)
        carried = dot(high_low, high1)
        other_half = high.at[1 - core]
        remote(other_half, other_half, high_sems.at[0], high_sems.at[1], partner).wait_recv()
        inv_high[...] = high2
        out_high[...] = nt(inv_high[share_rows, :], high[1] - nt(high[0], carried))

    for copy in pairs:
        copy.wait_send()
    for n in range(3):
        all_shares(n).wait_send()

    @pl.when(sub == 1)
    def _():
        each_peer(lambda i: p1_piece(i).wait_send())
        each_peer(lambda i: p2_piece(i).wait_send())

    @pl.when(sub == 0)
    def _():
        each_peer(lambda i: lead_piece(i).wait_send())

    @pl.when(core == 0)
    def _():
        root_copy.wait_send()
        for copy in c1_copies:
            copy.wait_send()

    @pl.when(core == 1)
    def _():
        pl.when(upper == 0)(c2_copy.wait_send)
        pl.when(upper == 1)(q2_copy.wait_send)

    pl.when(upper == 1)(high_copy.wait_send)
    for copy, wanted in child_copies:
        pl.when(wanted)(copy.wait_send)


def body(leaf_update, maps_low, maps_high):
    dma = pltpu.SemaphoreType.DMA

    def vmem(*shape):
        return pltpu.VMEM(shape, jnp.float32)

    low, high = pl.pallas_call(
        kernel,
        out_shape=(
            jax.ShapeDtypeStruct((1, SEP, HALF), jnp.float32),
            jax.ShapeDtypeStruct((HALF // 2, SEP), jnp.float32),
        ),
        in_specs=[pl.BlockSpec(memory_space=pl.ANY)] * 3,
        out_specs=(pl.BlockSpec(memory_space=pltpu.VMEM), pl.BlockSpec(memory_space=pltpu.VMEM)),
        scratch_shapes=[
            vmem(SEP, 2 * SEP), vmem(SEP, 2 * SEP), vmem(SEP, 2 * SEP),
            vmem(HALF, HALF), vmem(HALF, SEP), vmem(HALF, 2 * SEP),
            vmem(SEP, SEP), vmem(HALF, SEP), vmem(HALF, SEP), vmem(2, SEP, HALF),
            vmem(2, HALF, HALF), vmem(2, HALF, SEP), vmem(HALF, SEP), vmem(4, SEP, HALF), vmem(2, SEP, HALF),
            vmem(HALF, HALF),
            pltpu.SMEM((32, 32), jnp.int32), pltpu.SMEM((16, 32), jnp.int32), dma((2,)), dma((3,)), dma((2, 3)),
            dma((BLOCKS,)), dma((BLOCKS,)), dma((BLOCKS,)), dma((3,)), dma((3,)), dma((3,)),
            dma((2,)), dma((3,)), dma((2,)), dma((2,)), dma((2,)), dma((3,)), dma((4,)), dma((2,)),
        ],
        compiler_params=pltpu.CompilerParams(
            collective_id=0, has_side_effects=True, vmem_limit_bytes=64 * 1024 * 1024
        ),
        cost_estimate=pl.CostEstimate(flops=2_000_000_000, bytes_accessed=1_000_000, transcendentals=0),
    )(maps_low, maps_high, leaf_update)
    return low, high.T[None]


def solution(mesh):
    in_specs = (P("cube", "sub", None), P(), P())
    out_specs = (P("cube", "sub", None), P("cube", "sub", None))
    return jax.shard_map(body, mesh=mesh, in_specs=in_specs, out_specs=out_specs, check_vma=False)
```

```python
import jax
import jax.numpy as jnp
from jax import lax
from jax.experimental import pallas as pl
from jax.experimental.pallas import tpu as pltpu
from jax.sharding import PartitionSpec as P

SEP = 256
HALF = 128
BLOCKS = 16
BAND = 4
P2_STEP = 10
ROWS_STEP = 1
LEAD_STEP = 8
OWN_STEP = 11
BOTH_STEP = 14
HIGHEST = lax.Precision.HIGHEST
MESH = pl.DeviceIdType.MESH


def dot(a, b):
    return jnp.dot(a, b, precision=HIGHEST, preferred_element_type=jnp.float32)


def pieces(x):
    high = x.astype(jnp.bfloat16)
    rest = x - high.astype(jnp.float32)
    mid = rest.astype(jnp.bfloat16)
    return high, mid, (rest - mid.astype(jnp.float32)).astype(jnp.bfloat16)


def stacked(a, b, a_axis, b_axis):
    ah, am, al = pieces(a)
    bh, bm, bl = pieces(b)
    return lax.dot_general(
        jnp.concatenate([ah, ah, am, am, ah, al], axis=a_axis),
        jnp.concatenate([bh, bm, bh, bm, bl, bh], axis=b_axis),
        (((a_axis,), (b_axis,)), ((), ())),
        preferred_element_type=jnp.float32,
    )


def nt(a, b):
    return stacked(a, b, 1, 1)


def lane(x, c):
    return jnp.broadcast_to(x[:, c : c + 1], (x.shape[0], HALF))


def row(x, j):
    return jnp.broadcast_to(x[j : j + 1, :], (8, HALF))


def scaled(x, r):
    n = x.shape[0]
    return (x.reshape(n // 8, 8, HALF) * r[None]).reshape(n, HALF)


def inverse_factor(block, hooks=None):
    n = block.shape[0]
    steps = n // 8
    sublane = lax.broadcasted_iota(jnp.int32, (8, HALF), 0)
    eye = (
        lax.broadcasted_iota(jnp.int32, (n, n), 0) == lax.broadcasted_iota(jnp.int32, (n, n), 1)
    ).astype(jnp.float32)
    near = 8 * (BAND + 1)
    trail, far = block[:near], block[near:]
    unit, far_unit = eye[:near], eye[near:]
    done = []
    head = [lane(trail[:8], j) for j in range(8)]
    for k in range(steps):
        if hooks and k in hooks:
            hooks[k]()
        c0 = 8 * k
        t_head, t_tail = trail[:8], trail[8:]
        u_head, u_tail = unit[:8], unit[8:]
        last = k == steps - 1
        if k % BAND == 0:
            band_rows, band_unit = [], []
        if not last:
            tail = [lane(t_tail, c0 + j) for j in range(8)]
            ahead = [lane(t_tail[:8], c0 + 8 + j) for j in range(8)]
        pivots = None
        for j in range(8):
            pivot = row(head[j], j)
            inv = 1.0 / pivot
            head_inv = head[j] * inv
            for q in range(j + 1, 8):
                m = row(head[q], j) * inv if q == j + 1 else row(head_inv, q)
                head[q] = head[q] - head[j] * m
                if not last:
                    tail[q] = tail[q] - scaled(tail[j], m)
            below = jnp.where(sublane > j, head[j], 0.0)
            u_row = row(u_head, j) * inv
            u_head = u_head - below * u_row
            if not last:
                first = tail[j][:8]
                first_inv = first * inv
                for q in range(8):
                    ahead[q] = ahead[q] - first * row(first_inv, q)
                t_row = row(t_head, j) * inv
                t_head = t_head - below * t_row
                t_tail = t_tail - scaled(tail[j], t_row)
                u_tail = u_tail - scaled(tail[j], u_row)
            pivots = pivot if pivots is None else jnp.where(sublane == j, pivot, pivots)
        scale = lax.rsqrt(pivots)
        done.append(u_head * scale)
        if last:
            break
        band_rows.append(t_head * scale)
        band_unit.append(done[-1])
        trail, unit, head = t_tail, u_tail, ahead
        if k % BAND == BAND - 1 and far is not None:
            top = n - far.shape[0]
            rows_done = jnp.concatenate(band_rows, axis=0)
            ahead_rows = rows_done[:, top:]
            far = far - stacked(ahead_rows, rows_done, 0, 0)
            far_unit = far_unit - stacked(ahead_rows, jnp.concatenate(band_unit, axis=0), 0, 0)
            take = min(8 * BAND, n - top)
            trail = jnp.concatenate([trail, far[:take]], axis=0)
            unit = jnp.concatenate([unit, far_unit[:take]], axis=0)
            far, far_unit = (far[take:], far_unit[take:]) if top + take < n else (None, None)
    return jnp.concatenate(done, axis=0)


def kernel(
    maps_low, maps_high, leaf, out_low, out_high,
    slab, slab_in, front, p1_stage, p1, p2, lead, root, root_in, panel, c1, c2, q2, child, high, inv_high, left, pending, result,
    low_table, high_table, table_sems, load_sems, pair_sems,
    p1_cut, p2_cut, lead_cut, gather_send, gather_recv, piece_recv, stage_recv, p2_pair, out_sems,
    root_sems, c1_send, c1_recv, c2_sems, q2_sems, child_send, child_recv, high_sems,
):
    cube = lax.axis_index("cube")
    sub = lax.axis_index("sub")
    node = cube // 2
    core = cube % 2
    upper = node % 2
    other = node + 1 - 2 * upper
    partner = (cube + 1 - 2 * core, sub)
    across = (2 * other + core, sub)
    diagonal = (2 * other + 1 - core, sub)
    parts = ((SEP, HALF), (SEP + HALF, HALF), (0, SEP))

    def remote(src, dst, send_sem, recv_sem, device):
        return pltpu.make_async_remote_copy(
            src_ref=src, dst_ref=dst, send_sem=send_sem, recv_sem=recv_sem, device_id=device, device_id_type=MESH
        )

    def rows(i, base=0):
        return pl.ds(pl.multiple_of(base + 8 * i, 8), 8)

    def each_peer(fn):
        def step(t, carry):
            fn((sub + t) % BLOCKS)
            return carry

        lax.fori_loop(1, BLOCKS, step, 0)

    loads = [
        pltpu.make_async_copy(leaf.at[0, :, pl.ds(*part)], slab.at[:, pl.ds(*part)], load_sems.at[i])
        for i, part in enumerate(parts)
    ]
    tables = [
        pltpu.make_async_copy(maps_low, low_table, table_sems.at[0]),
        pltpu.make_async_copy(maps_high, high_table, table_sems.at[1]),
    ]
    for copy in loads + tables:
        copy.start()

    barrier = pltpu.get_barrier_semaphore()

    def greet(device):
        pl.semaphore_signal(barrier, inc=1, device_id=device, device_id_type=MESH)

    for device in (partner, across, diagonal):
        greet(device)
    each_peer(lambda i: greet((cube, i)))
    pl.when(sub != 1)(lambda: greet((partner[0], 1)))
    pl.when(sub != 1)(lambda: pl.semaphore_wait(barrier, BLOCKS + 2))
    pl.when(sub == 1)(lambda: pl.semaphore_wait(barrier, 2 * BLOCKS + 1))

    def p1_piece(cube_to, i):
        return remote(slab.at[rows(i), pl.ds(SEP, HALF)], p1_stage.at[core], p1_cut, stage_recv.at[core], (cube_to, i))

    loads[0].wait()

    @pl.when(sub == 1)
    def _():
        def both(i):
            p1_piece(cube, i).start()
            p1_piece(partner[0], i).start()

        each_peer(both)
        p1_piece(partner[0], sub).start()
        p1_stage[core] = slab[rows(sub), SEP : SEP + HALF]


    pairs = [
        remote(slab.at[:, pl.ds(*part)], slab_in.at[:, pl.ds(*part)], pair_sems.at[0, i], pair_sems.at[1, i], partner)
        for i, part in enumerate(parts)
    ]
    pairs[0].start()
    for load, copy in zip(loads[1:], pairs[1:]):
        load.wait()
        copy.start()
    for copy in tables:
        copy.wait()

    def tiles(block, table, index):
        moved = jnp.full((HALF, block.shape[1]), table[index, 2 * sub], jnp.int32) != 2 * sub
        first, second = block[:HALF, :], block[HALF:, :]
        return jnp.where(moved, second, first), jnp.where(moved, first, second)

    def extend_add(i):
        pairs[i].wait_recv()
        cols = slice(parts[i][0], sum(parts[i]))
        own = tiles(slab[:, cols], low_table, cube)
        theirs = tiles(slab_in[:, cols], low_table, cube + 1 - 2 * core)
        front[:HALF, cols] = own[0] + theirs[0]
        front[HALF:, cols] = own[1] + theirs[1]

    p2_columns = pl.ds(pl.multiple_of(SEP + core * HALF, HALF), HALF)

    def p2_piece(i):
        return remote(front.at[rows(i, HALF), p2_columns], p2.at[core, rows(i)], p2_cut.at[i], piece_recv.at[1], (cube, i))

    def lead_piece(i):
        return remote(front.at[rows(i, core * HALF)], lead.at[rows(i)], lead_cut.at[i], piece_recv.at[2], (cube, i))

    blocks = (p1, p2.at[core], lead)

    def share(n, i):
        own = blocks[n].at[rows(sub)]
        return remote(own, own, gather_send.at[n], gather_recv.at[n], (cube, i))

    def pass_on(n, owner):
        own = blocks[n].at[rows(sub)]

        @pl.when(sub != owner)
        def _():
            remote(own, own, gather_send.at[n], piece_recv.at[n], (cube, owner)).wait_recv()

        each_peer(lambda i: share(n, i).start())

    def all_shares(n):
        others = blocks[n].at[pl.ds(0, 8 * (BLOCKS - 1))]
        return remote(others, others, gather_send.at[n], gather_recv.at[n], partner)

    extend_add(0)
    extend_add(1)

    @pl.when(sub == 1)
    def _():
        each_peer(lambda i: p2_piece(i).start())
        p2[core, rows(sub), :] = front[rows(sub, HALF), p2_columns]

    extend_add(2)

    @pl.when(sub == 0)
    def _():
        each_peer(lambda i: lead_piece(i).start())
        lead[rows(sub), :] = front[rows(sub, core * HALF), :]

    for c in range(2):
        @pl.when(jnp.logical_or(sub != 1, core != c))
        def _():
            remote(p1_stage.at[c], p1_stage.at[c], p1_cut, stage_recv.at[c], partner).wait_recv()

    p1[rows(sub), :] = p1_stage[0] + p1_stage[1]
    each_peer(lambda i: share(0, i).start())
    pass_on(1, 1)
    pass_on(2, 0)

    all_shares(0).wait_recv()
    p2_copy = remote(p2.at[core], p2.at[core], p2_pair.at[0], p2_pair.at[1], partner)

    def p2_half():
        all_shares(1).wait_recv()
        p2_copy.start()

    inv1 = inverse_factor(p1[...], {P2_STEP: p2_half})
    p2_other = p2.at[1 - core]
    remote(p2_other, p2_other, p2_pair.at[0], p2_pair.at[1], partner).wait_recv()
    low = nt(p2[0], inv1)
    root_copies = [
        remote(root.at[:, part], root_in.at[:, part], root_sems.at[0, i], root_sems.at[1, i], partner)
        for i, part in enumerate((pl.ds(0, HALF), pl.ds(HALF, HALF)))
    ]

    def first_root():
        all_shares(2).wait_recv()
        root1 = nt(lead[:, SEP : SEP + HALF], inv1)
        root[:, :HALF] = root1
        pl.when(core == 0)(root_copies[0].start)
        left[0] = lead[:, SEP + HALF :] - nt(root1, low)
        left[1] = lead[:, pl.ds(pl.multiple_of(core * HALF, HALF), HALF)] - nt(root1, root1)

        child[core] = own_columns - nt(panel[0], root1)

    own_columns = front[:, pl.ds(pl.multiple_of(core * HALF, HALF), HALF)]

    def first_panel():
        panel[0] = nt(front[:, SEP : SEP + HALF], inv1)
        panel[1] = front[:, SEP + HALF :] - nt(panel[0], low)

    inv2 = inverse_factor(p2[1] - nt(low, low), {ROWS_STEP: first_panel, LEAD_STEP: first_root})
    root2 = nt(left[0], inv2)
    root[:, HALF:] = root2
    c1_copies = [
        remote(c1.at[0], c1.at[slot], c1_send.at[i], c1_recv.at[slot], device)
        for i, (slot, device) in enumerate(((0, partner), (1, across), (1, diagonal)))
    ]
    c2_copies = [
        remote(c2.at[0, part], c2.at[1, part], c2_sems.at[0, part], c2_sems.at[1, part], across) for part in range(2)
    ]

    @pl.when(core == 0)
    def _():
        root_copies[1].start()
        c1[0] = left[1] - nt(root2, root2)
        for copy in reversed(c1_copies):
            copy.start()

    @pl.when(core == 1)
    def _():
        c2[0, 1] = left[1] - nt(root2, root2)
        pl.when(upper == 0)(c2_copies[1].start)
        root_copies[0].wait_recv()
        across1 = nt(root[:, :HALF], root_in[:, :HALF])
        root_copies[1].wait_recv()
        c2[0, 0] = lead[:, :HALF] - across1 - nt(root2, root_in[:, HALF:])
        pl.when(upper == 0)(c2_copies[0].start)

    keep = (sub != 1).astype(jnp.float32)
    w2 = nt(panel[1], inv2)
    panel[1] = w2
    child[core] = (child[core] - nt(w2, root2)) * keep
    mine, theirs = child.at[core], child.at[2 + core]
    child_copies = [
        (remote(mine, theirs, child_send.at[0], child_recv.at[2 + core], across), jnp.logical_or(core == 0, upper == 0)),
        (remote(mine, mine, child_send.at[1], child_recv.at[core], partner), jnp.logical_and(core == 0, upper == 0)),
        (remote(mine, theirs, child_send.at[2], child_recv.at[2 + core], diagonal), jnp.logical_and(core == 0, upper == 1)),
    ]
    for copy, wanted in child_copies:
        pl.when(wanted)(copy.start)
    out_copies = [
        pltpu.make_async_copy(panel.at[core], out_low.at[0], out_sems.at[0]),
        pltpu.make_async_copy(result, out_high, out_sems.at[1]),
    ]
    out_copies[0].start()

    pl.when(core == 1)(c1_copies[0].wait_recv)
    c1_copies[1].wait_recv()
    high1 = inverse_factor(c1[0] + c1[1])
    inv_high[...] = high1
    share_rows = pl.ds(pl.multiple_of(core * 64, 64), 64)

    def child_wait(slot):
        remote(child.at[slot], child.at[slot], child_send.at[0], child_recv.at[slot], partner).wait_recv()

    def high_columns(half):
        own = tiles(child[half], high_table, node)
        theirs = tiles(child[2 + half], high_table, other)
        return jnp.concatenate([own[0] + theirs[0], own[1] + theirs[1]], axis=0)

    q2_copies = [remote(q2.at[part], q2.at[part], q2_sems.at[0, part], q2_sems.at[1, part], partner) for part in range(2)]
    high_copy = remote(high.at[core], high.at[core], high_sems.at[0], high_sems.at[1], partner)

    @pl.when(upper == 0)
    def _():
        pl.when(core == 1)(lambda: child_wait(0))
        child_wait(2)
        result[...] = nt(inv_high[share_rows, :], high_columns(0))

    @pl.when(upper == 1)
    def _():
        @pl.when(core == 1)
        def _():
            for part in (1, 0):
                c2_copies[part].wait_recv()
                q2[part] = c2[0, part] + c2[1, part]
                q2_copies[part].start()

        @pl.when(core == 0)
        def _():
            for part in (1, 0):
                q2_copies[part].wait_recv()

        high_low = nt(q2[0], high1)

        def own_high():
            child_wait(2 + core)
            high[core] = high_columns(core)
            high_copy.start()

        carried = dot(high_low, high1)
        other_half = high.at[1 - core]

        def both_high():
            remote(other_half, other_half, high_sems.at[0], high_sems.at[1], partner).wait_recv()
            pending[...] = high[1] - nt(high[0], carried)

        high2 = inverse_factor(q2[1] - nt(high_low, high_low), {OWN_STEP: own_high, BOTH_STEP: both_high})
        inv_high[...] = high2
        result[...] = nt(inv_high[share_rows, :], pending[...])

    out_copies[1].start()

    for copy in (*pairs, p2_copy):
        copy.wait_send()
    for n in range(3):
        all_shares(n).wait_send()

    @pl.when(sub == 1)
    def _():
        sent = slab_in.at[pl.ds(0, 8 * (2 * BLOCKS - 1)), pl.ds(0, HALF)]
        remote(sent, sent, p1_cut, stage_recv.at[0], partner).wait_send()
        each_peer(lambda i: p2_piece(i).wait_send())

    @pl.when(sub == 0)
    def _():
        each_peer(lambda i: lead_piece(i).wait_send())

    @pl.when(core == 0)
    def _():
        for copy in root_copies:
            copy.wait_send()
        for copy in c1_copies:
            copy.wait_send()

    @pl.when(core == 1)
    def _():
        for part in range(2):
            pl.when(upper == 0)(c2_copies[part].wait_send)
            pl.when(upper == 1)(q2_copies[part].wait_send)

    pl.when(upper == 1)(high_copy.wait_send)
    for copy, wanted in child_copies:
        pl.when(wanted)(copy.wait_send)
    for copy in out_copies:
        copy.wait()


def place(low, high, out_low, out_high):
    out_low[...] = low[...]
    out_high[...] = high[...]


def body(leaf_update, maps_low, maps_high):
    dma = pltpu.SemaphoreType.DMA

    def vmem(*shape):
        return pltpu.VMEM(shape, jnp.float32)

    low, high = pl.pallas_call(
        kernel,
        out_shape=(
            jax.ShapeDtypeStruct((1, SEP, HALF), jnp.float32),
            jax.ShapeDtypeStruct((HALF // 2, SEP), jnp.float32),
        ),
        in_specs=[pl.BlockSpec(memory_space=pl.ANY)] * 3,
        out_specs=(pl.BlockSpec(memory_space=pl.ANY),) * 2,
        scratch_shapes=[
            vmem(SEP, 2 * SEP), vmem(SEP, 2 * SEP), vmem(SEP, 2 * SEP),
            vmem(2, 8, HALF), vmem(HALF, HALF), vmem(2, HALF, HALF), vmem(HALF, 2 * SEP),
            vmem(HALF, SEP), vmem(HALF, SEP), vmem(2, SEP, HALF),
            vmem(2, HALF, HALF), vmem(2, 2, HALF, HALF), vmem(2, HALF, HALF), vmem(4, SEP, HALF), vmem(2, SEP, HALF),
            vmem(HALF, HALF), vmem(2, HALF, HALF), vmem(SEP, HALF), vmem(HALF // 2, SEP),
            pltpu.SMEM((32, 32), jnp.int32), pltpu.SMEM((16, 32), jnp.int32), dma((2,)), dma((3,)), dma((2, 3)),
            dma, dma((BLOCKS,)), dma((BLOCKS,)), dma((3,)), dma((3,)), dma((3,)), dma((2,)), dma((2,)), dma((2,)),
            dma((2, 2)), dma((3,)), dma((2,)), dma((2, 2)), dma((2, 2)), dma((3,)), dma((4,)), dma((2,)),
        ],
        compiler_params=pltpu.CompilerParams(
            collective_id=0, has_side_effects=True, vmem_limit_bytes=64 * 1024 * 1024
        ),
        cost_estimate=pl.CostEstimate(flops=2_000_000_000, bytes_accessed=1_000_000, transcendentals=0),
    )(maps_low, maps_high, leaf_update)
    low, high = pl.pallas_call(
        place,
        out_shape=(jax.ShapeDtypeStruct(low.shape, low.dtype), jax.ShapeDtypeStruct(high.shape, high.dtype)),
        in_specs=[pl.BlockSpec(memory_space=pltpu.VMEM)] * 2,
        out_specs=(pl.BlockSpec(memory_space=pltpu.VMEM),) * 2,
    )(low, high)
    return low, high.T[None]


def solution(mesh):
    in_specs = (P("cube", "sub", None), P(), P())
    out_specs = (P("cube", "sub", None), P("cube", "sub", None))
    return jax.shard_map(body, mesh=mesh, in_specs=in_specs, out_specs=out_specs, check_vma=False)
```

```python
import jax
import jax.numpy as jnp
from jax import lax
from jax.experimental import pallas as pl
from jax.experimental.pallas import tpu as pltpu
from jax.sharding import PartitionSpec as P

SEP = 256
HALF = 128
BLOCKS = 16
BAND = 4
P2_STEP = 13
ROWS_STEP = 1
LEAD_STEP = 10
OWN_STEP = 13
BOTH_STEP = 15
HIGHEST = lax.Precision.HIGHEST
MESH = pl.DeviceIdType.MESH


def dot(a, b):
    return jnp.dot(a, b, precision=HIGHEST, preferred_element_type=jnp.float32)


def pieces(x):
    high = x.astype(jnp.bfloat16)
    rest = x - high.astype(jnp.float32)
    mid = rest.astype(jnp.bfloat16)
    return high, mid, (rest - mid.astype(jnp.float32)).astype(jnp.bfloat16)


def stacked(a, b, a_axis, b_axis):
    ah, am, al = pieces(a)
    bh, bm, bl = pieces(b)
    return lax.dot_general(
        jnp.concatenate([ah, ah, am, am, ah, al], axis=a_axis),
        jnp.concatenate([bh, bm, bh, bm, bl, bh], axis=b_axis),
        (((a_axis,), (b_axis,)), ((), ())),
        preferred_element_type=jnp.float32,
    )


def nt(a, b):
    return stacked(a, b, 1, 1)


def lane(x, c):
    return jnp.broadcast_to(x[:, c : c + 1], (x.shape[0], HALF))


def row(x, j):
    return jnp.broadcast_to(x[j : j + 1, :], (8, HALF))


def scaled(x, r):
    n = x.shape[0]
    return (x.reshape(n // 8, 8, HALF) * r[None]).reshape(n, HALF)


def inverse_factor(block, hooks=None):
    n = block.shape[0]
    steps = n // 8
    sublane = lax.broadcasted_iota(jnp.int32, (8, HALF), 0)
    eye = (
        lax.broadcasted_iota(jnp.int32, (n, n), 0) == lax.broadcasted_iota(jnp.int32, (n, n), 1)
    ).astype(jnp.float32)
    near = 8 * (BAND + 1)
    trail, far = block[:near], block[near:]
    unit, far_unit = eye[:near], eye[near:]
    done = []
    head = [lane(trail[:8], j) for j in range(8)]
    for k in range(steps):
        if hooks and k in hooks:
            hooks[k]()
        c0 = 8 * k
        t_head, t_tail = trail[:8], trail[8:]
        u_head, u_tail = unit[:8], unit[8:]
        last = k == steps - 1
        if k % BAND == 0:
            band_rows, band_unit = [], []
        if not last:
            tail = [lane(t_tail, c0 + j) for j in range(8)]
            ahead = [lane(t_tail[:8], c0 + 8 + j) for j in range(8)]
        pivots = None
        for j in range(8):
            pivot = row(head[j], j)
            inv = 1.0 / pivot
            head_inv = head[j] * inv
            for q in range(j + 1, 8):
                m = row(head[q], j) * inv if q == j + 1 else row(head_inv, q)
                head[q] = head[q] - head[j] * m
                if not last:
                    tail[q] = tail[q] - scaled(tail[j], m)
            below = jnp.where(sublane > j, head[j], 0.0)
            u_row = row(u_head, j) * inv
            u_head = u_head - below * u_row
            if not last:
                first = tail[j][:8]
                first_inv = first * inv
                for q in range(8):
                    ahead[q] = ahead[q] - first * row(first_inv, q)
                t_row = row(t_head, j) * inv
                t_head = t_head - below * t_row
                t_tail = t_tail - scaled(tail[j], t_row)
                u_tail = u_tail - scaled(tail[j], u_row)
            pivots = pivot if pivots is None else jnp.where(sublane == j, pivot, pivots)
        scale = lax.rsqrt(pivots)
        done.append(u_head * scale)
        if last:
            break
        band_rows.append(t_head * scale)
        band_unit.append(done[-1])
        trail, unit, head = t_tail, u_tail, ahead
        if k % BAND == BAND - 1 and far is not None:
            top = n - far.shape[0]
            rows_done = jnp.concatenate(band_rows, axis=0)
            both = jnp.concatenate([rows_done, jnp.concatenate(band_unit, axis=0)], axis=1)
            change = stacked(rows_done, both, 0, 0)[top:]
            far, far_unit = far - change[:, :n], far_unit - change[:, n:]
            take = min(8 * BAND, n - top)
            trail = jnp.concatenate([trail, far[:take]], axis=0)
            unit = jnp.concatenate([unit, far_unit[:take]], axis=0)
            far, far_unit = (far[take:], far_unit[take:]) if top + take < n else (None, None)
    return jnp.concatenate(done, axis=0)


def kernel(
    maps_low, maps_high, leaf, out_low, out_high,
    slab, slab_in, front, p1_stage, p1, p2, lead, root, root_in, panel, c1, c2, q2, child, high, inv_high, left, pending, result,
    low_table, high_table, table_sems, load_sems, pair_sems,
    p1_cut, p2_cut, lead_cut, gather_send, gather_recv, piece_recv, stage_recv, p2_pair, out_sems,
    root_sems, c1_send, c1_recv, c2_sems, q2_sems, child_send, child_recv, high_sems,
):
    cube = lax.axis_index("cube")
    sub = lax.axis_index("sub")
    node = cube // 2
    core = cube % 2
    upper = node % 2
    other = node + 1 - 2 * upper
    partner = (cube + 1 - 2 * core, sub)
    across = (2 * other + core, sub)
    diagonal = (2 * other + 1 - core, sub)
    parts = ((SEP, HALF), (SEP + HALF, HALF), (0, SEP))

    def remote(src, dst, send_sem, recv_sem, device):
        return pltpu.make_async_remote_copy(
            src_ref=src, dst_ref=dst, send_sem=send_sem, recv_sem=recv_sem, device_id=device, device_id_type=MESH
        )

    def rows(i, base=0):
        return pl.ds(pl.multiple_of(base + 8 * i, 8), 8)

    def each_peer(fn):
        def step(t, carry):
            fn((sub + t) % BLOCKS)
            return carry

        lax.fori_loop(1, BLOCKS, step, 0)

    loads = [
        pltpu.make_async_copy(leaf.at[0, :, pl.ds(*part)], slab.at[:, pl.ds(*part)], load_sems.at[i])
        for i, part in enumerate(parts)
    ]
    tables = [
        pltpu.make_async_copy(maps_low, low_table, table_sems.at[0]),
        pltpu.make_async_copy(maps_high, high_table, table_sems.at[1]),
    ]
    for copy in loads + tables:
        copy.start()

    barrier = pltpu.get_barrier_semaphore()

    def greet(device):
        pl.semaphore_signal(barrier, inc=1, device_id=device, device_id_type=MESH)

    for device in (partner, across, diagonal):
        greet(device)
    each_peer(lambda i: greet((cube, i)))
    pl.when(sub != 1)(lambda: greet((partner[0], 1)))
    pl.when(sub != 1)(lambda: pl.semaphore_wait(barrier, BLOCKS + 2))
    pl.when(sub == 1)(lambda: pl.semaphore_wait(barrier, 2 * BLOCKS + 1))

    def p1_piece(cube_to, i):
        return remote(slab.at[rows(i), pl.ds(SEP, HALF)], p1_stage.at[core], p1_cut, stage_recv.at[core], (cube_to, i))

    loads[0].wait()

    @pl.when(sub == 1)
    def _():
        def both(i):
            p1_piece(cube, i).start()
            p1_piece(partner[0], i).start()

        each_peer(both)
        p1_piece(partner[0], sub).start()
        p1_stage[core] = slab[rows(sub), SEP : SEP + HALF]


    pairs = [
        remote(slab.at[:, pl.ds(*part)], slab_in.at[:, pl.ds(*part)], pair_sems.at[0, i], pair_sems.at[1, i], partner)
        for i, part in enumerate(parts)
    ]
    pairs[0].start()
    for load, copy in zip(loads[1:], pairs[1:]):
        load.wait()
        copy.start()
    for copy in tables:
        copy.wait()

    def tiles(block, table, index):
        moved = jnp.full((HALF, block.shape[1]), table[index, 2 * sub], jnp.int32) != 2 * sub
        first, second = block[:HALF, :], block[HALF:, :]
        return jnp.where(moved, second, first), jnp.where(moved, first, second)

    def extend_add(i):
        pairs[i].wait_recv()
        cols = slice(parts[i][0], sum(parts[i]))
        own = tiles(slab[:, cols], low_table, cube)
        theirs = tiles(slab_in[:, cols], low_table, cube + 1 - 2 * core)
        front[:HALF, cols] = own[0] + theirs[0]
        front[HALF:, cols] = own[1] + theirs[1]

    p2_columns = pl.ds(pl.multiple_of(SEP + core * HALF, HALF), HALF)

    def p2_piece(i):
        return remote(front.at[rows(i, HALF), p2_columns], p2.at[core, rows(i)], p2_cut.at[i], piece_recv.at[1], (cube, i))

    def lead_piece(i):
        return remote(front.at[rows(i, core * HALF)], lead.at[rows(i)], lead_cut.at[i], piece_recv.at[2], (cube, i))

    blocks = (p1, p2.at[core], lead)

    def share(n, i):
        own = blocks[n].at[rows(sub)]
        return remote(own, own, gather_send.at[n], gather_recv.at[n], (cube, i))

    def pass_on(n, owner):
        own = blocks[n].at[rows(sub)]

        @pl.when(sub != owner)
        def _():
            remote(own, own, gather_send.at[n], piece_recv.at[n], (cube, owner)).wait_recv()

        each_peer(lambda i: share(n, i).start())

    def all_shares(n):
        others = blocks[n].at[pl.ds(0, 8 * (BLOCKS - 1))]
        return remote(others, others, gather_send.at[n], gather_recv.at[n], partner)

    extend_add(0)
    extend_add(1)

    @pl.when(sub == 1)
    def _():
        each_peer(lambda i: p2_piece(i).start())
        p2[core, rows(sub), :] = front[rows(sub, HALF), p2_columns]

    extend_add(2)

    @pl.when(sub == 0)
    def _():
        each_peer(lambda i: lead_piece(i).start())
        lead[rows(sub), :] = front[rows(sub, core * HALF), :]

    for c in range(2):
        @pl.when(jnp.logical_or(sub != 1, core != c))
        def _():
            remote(p1_stage.at[c], p1_stage.at[c], p1_cut, stage_recv.at[c], partner).wait_recv()

    p1[rows(sub), :] = p1_stage[0] + p1_stage[1]
    each_peer(lambda i: share(0, i).start())
    pass_on(1, 1)
    pass_on(2, 0)

    all_shares(0).wait_recv()
    p2_copy = remote(p2.at[core], p2.at[core], p2_pair.at[0], p2_pair.at[1], partner)

    def p2_half():
        all_shares(1).wait_recv()
        p2_copy.start()

    inv1 = inverse_factor(p1[...], {P2_STEP: p2_half})
    p2_other = p2.at[1 - core]
    remote(p2_other, p2_other, p2_pair.at[0], p2_pair.at[1], partner).wait_recv()
    low = nt(p2[0], inv1)
    root_copies = [
        remote(root.at[:, part], root_in.at[:, part], root_sems.at[0, i], root_sems.at[1, i], partner)
        for i, part in enumerate((pl.ds(0, HALF), pl.ds(HALF, HALF)))
    ]

    def first_root():
        all_shares(2).wait_recv()
        root1 = nt(lead[:, SEP : SEP + HALF], inv1)
        root[:, :HALF] = root1
        pl.when(core == 0)(root_copies[0].start)
        left[0] = lead[:, SEP + HALF :] - nt(root1, low)
        left[1] = lead[:, pl.ds(pl.multiple_of(core * HALF, HALF), HALF)] - nt(root1, root1)

        child[core] = own_columns - nt(panel[0], root1)

    own_columns = front[:, pl.ds(pl.multiple_of(core * HALF, HALF), HALF)]

    def first_panel():
        panel[0] = nt(front[:, SEP : SEP + HALF], inv1)
        panel[1] = front[:, SEP + HALF :] - nt(panel[0], low)

    inv2 = inverse_factor(p2[1] - nt(low, low), {ROWS_STEP: first_panel, LEAD_STEP: first_root})
    root2 = nt(left[0], inv2)
    root[:, HALF:] = root2
    c1_copies = [
        remote(c1.at[0], c1.at[slot], c1_send.at[i], c1_recv.at[slot], device)
        for i, (slot, device) in enumerate(((0, partner), (1, across), (1, diagonal)))
    ]
    c2_copies = [
        remote(c2.at[0, part], c2.at[1, part], c2_sems.at[0, part], c2_sems.at[1, part], across) for part in range(2)
    ]

    @pl.when(core == 0)
    def _():
        root_copies[1].start()
        c1[0] = left[1] - nt(root2, root2)
        for copy in reversed(c1_copies):
            copy.start()

    @pl.when(core == 1)
    def _():
        c2[0, 1] = left[1] - nt(root2, root2)
        pl.when(upper == 0)(c2_copies[1].start)
        root_copies[0].wait_recv()
        across1 = nt(root[:, :HALF], root_in[:, :HALF])
        root_copies[1].wait_recv()
        c2[0, 0] = lead[:, :HALF] - across1 - nt(root2, root_in[:, HALF:])
        pl.when(upper == 0)(c2_copies[0].start)

    keep = (sub != 1).astype(jnp.float32)
    w2 = nt(panel[1], inv2)
    panel[1] = w2
    child[core] = (child[core] - nt(w2, root2)) * keep
    mine, theirs = child.at[core], child.at[2 + core]
    child_copies = [
        (remote(mine, theirs, child_send.at[0], child_recv.at[2 + core], across), jnp.logical_or(core == 0, upper == 0)),
        (remote(mine, mine, child_send.at[1], child_recv.at[core], partner), jnp.logical_and(core == 0, upper == 0)),
        (remote(mine, theirs, child_send.at[2], child_recv.at[2 + core], diagonal), jnp.logical_and(core == 0, upper == 1)),
    ]
    for copy, wanted in child_copies:
        pl.when(wanted)(copy.start)
    out_copies = [
        pltpu.make_async_copy(panel.at[core], out_low.at[0], out_sems.at[0]),
        pltpu.make_async_copy(result, out_high, out_sems.at[1]),
    ]
    out_copies[0].start()

    pl.when(core == 1)(c1_copies[0].wait_recv)
    c1_copies[1].wait_recv()
    high1 = inverse_factor(c1[0] + c1[1])
    inv_high[...] = high1
    share_rows = pl.ds(pl.multiple_of(core * 64, 64), 64)

    def child_wait(slot):
        remote(child.at[slot], child.at[slot], child_send.at[0], child_recv.at[slot], partner).wait_recv()

    def high_columns(half):
        own = tiles(child[half], high_table, node)
        theirs = tiles(child[2 + half], high_table, other)
        return jnp.concatenate([own[0] + theirs[0], own[1] + theirs[1]], axis=0)

    q2_copies = [remote(q2.at[part], q2.at[part], q2_sems.at[0, part], q2_sems.at[1, part], partner) for part in range(2)]
    high_copy = remote(high.at[core], high.at[core], high_sems.at[0], high_sems.at[1], partner)

    @pl.when(upper == 0)
    def _():
        pl.when(core == 1)(lambda: child_wait(0))
        child_wait(2)
        result[...] = nt(inv_high[share_rows, :], high_columns(0))

    @pl.when(upper == 1)
    def _():
        @pl.when(core == 1)
        def _():
            for part in (1, 0):
                c2_copies[part].wait_recv()
                q2[part] = c2[0, part] + c2[1, part]
                q2_copies[part].start()

        @pl.when(core == 0)
        def _():
            for part in (1, 0):
                q2_copies[part].wait_recv()

        high_low = nt(q2[0], high1)

        def own_high():
            child_wait(2 + core)
            high[core] = high_columns(core)
            high_copy.start()

        carried = dot(high_low, high1)
        other_half = high.at[1 - core]

        def both_high():
            remote(other_half, other_half, high_sems.at[0], high_sems.at[1], partner).wait_recv()
            pending[...] = high[1] - nt(high[0], carried)

        high2 = inverse_factor(q2[1] - nt(high_low, high_low), {OWN_STEP: own_high, BOTH_STEP: both_high})
        inv_high[...] = high2
        result[...] = nt(inv_high[share_rows, :], pending[...])

    out_copies[1].start()

    for copy in (*pairs, p2_copy):
        copy.wait_send()
    for n in range(3):
        all_shares(n).wait_send()

    @pl.when(sub == 1)
    def _():
        sent = slab_in.at[pl.ds(0, 8 * (2 * BLOCKS - 1)), pl.ds(0, HALF)]
        remote(sent, sent, p1_cut, stage_recv.at[0], partner).wait_send()
        each_peer(lambda i: p2_piece(i).wait_send())

    @pl.when(sub == 0)
    def _():
        each_peer(lambda i: lead_piece(i).wait_send())

    @pl.when(core == 0)
    def _():
        for copy in root_copies:
            copy.wait_send()
        for copy in c1_copies:
            copy.wait_send()

    @pl.when(core == 1)
    def _():
        for part in range(2):
            pl.when(upper == 0)(c2_copies[part].wait_send)
            pl.when(upper == 1)(q2_copies[part].wait_send)

    pl.when(upper == 1)(high_copy.wait_send)
    for copy, wanted in child_copies:
        pl.when(wanted)(copy.wait_send)
    for copy in out_copies:
        copy.wait()


def place(low, high, out_low, out_high):
    out_low[...] = low[...]
    out_high[...] = high[...]


def body(leaf_update, maps_low, maps_high):
    dma = pltpu.SemaphoreType.DMA

    def vmem(*shape):
        return pltpu.VMEM(shape, jnp.float32)

    low, high = pl.pallas_call(
        kernel,
        out_shape=(
            jax.ShapeDtypeStruct((1, SEP, HALF), jnp.float32),
            jax.ShapeDtypeStruct((HALF // 2, SEP), jnp.float32),
        ),
        in_specs=[pl.BlockSpec(memory_space=pl.ANY)] * 3,
        out_specs=(pl.BlockSpec(memory_space=pl.ANY),) * 2,
        scratch_shapes=[
            vmem(SEP, 2 * SEP), vmem(SEP, 2 * SEP), vmem(SEP, 2 * SEP),
            vmem(2, 8, HALF), vmem(HALF, HALF), vmem(2, HALF, HALF), vmem(HALF, 2 * SEP),
            vmem(HALF, SEP), vmem(HALF, SEP), vmem(2, SEP, HALF),
            vmem(2, HALF, HALF), vmem(2, 2, HALF, HALF), vmem(2, HALF, HALF), vmem(4, SEP, HALF), vmem(2, SEP, HALF),
            vmem(HALF, HALF), vmem(2, HALF, HALF), vmem(SEP, HALF), vmem(HALF // 2, SEP),
            pltpu.SMEM((32, 32), jnp.int32), pltpu.SMEM((16, 32), jnp.int32), dma((2,)), dma((3,)), dma((2, 3)),
            dma, dma((BLOCKS,)), dma((BLOCKS,)), dma((3,)), dma((3,)), dma((3,)), dma((2,)), dma((2,)), dma((2,)),
            dma((2, 2)), dma((3,)), dma((2,)), dma((2, 2)), dma((2, 2)), dma((3,)), dma((4,)), dma((2,)),
        ],
        compiler_params=pltpu.CompilerParams(
            collective_id=0, has_side_effects=True, vmem_limit_bytes=64 * 1024 * 1024
        ),
        cost_estimate=pl.CostEstimate(flops=2_000_000_000, bytes_accessed=1_000_000, transcendentals=0),
    )(maps_low, maps_high, leaf_update)
    low, high = pl.pallas_call(
        place,
        out_shape=(jax.ShapeDtypeStruct(low.shape, low.dtype), jax.ShapeDtypeStruct(high.shape, high.dtype)),
        in_specs=[pl.BlockSpec(memory_space=pltpu.VMEM)] * 2,
        out_specs=(pl.BlockSpec(memory_space=pltpu.VMEM),) * 2,
    )(low, high)
    return low, high.T[None]


def solution(mesh):
    in_specs = (P("cube", "sub", None), P(), P())
    out_specs = (P("cube", "sub", None), P("cube", "sub", None))
    return jax.shard_map(body, mesh=mesh, in_specs=in_specs, out_specs=out_specs, check_vma=False)
```

```python
import jax
import jax.numpy as jnp
from jax import lax
from jax.experimental import pallas as pl
from jax.experimental.pallas import tpu as pltpu
from jax.sharding import PartitionSpec as P

SEP = 256
HALF = 128
BLOCKS = 16
BAND = 4
P2_STEP = 13
ROWS_STEP = 1
LEAD_STEP = 10
OWN_STEP = 13
BOTH_STEP = 15
HIGHEST = lax.Precision.HIGHEST
MESH = pl.DeviceIdType.MESH


def dot(a, b):
    return jnp.dot(a, b, precision=HIGHEST, preferred_element_type=jnp.float32)


def pieces(x):
    high = x.astype(jnp.bfloat16)
    rest = x - high.astype(jnp.float32)
    mid = rest.astype(jnp.bfloat16)
    return high, mid, (rest - mid.astype(jnp.float32)).astype(jnp.bfloat16)


def stacked(a, b, a_axis, b_axis):
    ah, am, al = pieces(a)
    bh, bm, bl = pieces(b)
    return lax.dot_general(
        jnp.concatenate([ah, ah, am, am, ah, al], axis=a_axis),
        jnp.concatenate([bh, bm, bh, bm, bl, bh], axis=b_axis),
        (((a_axis,), (b_axis,)), ((), ())),
        preferred_element_type=jnp.float32,
    )


def nt(a, b):
    return stacked(a, b, 1, 1)


def lane(x, c):
    return jnp.broadcast_to(x[:, c : c + 1], (x.shape[0], HALF))


def row(x, j):
    return jnp.broadcast_to(x[j : j + 1, :], (8, HALF))


def scaled(x, r):
    n = x.shape[0]
    return (x.reshape(n // 8, 8, HALF) * r[None]).reshape(n, HALF)


def inverse_factor(block, hooks=None):
    n = block.shape[0]
    steps = n // 8
    sublane = lax.broadcasted_iota(jnp.int32, (8, HALF), 0)
    eye = (
        lax.broadcasted_iota(jnp.int32, (n, n), 0) == lax.broadcasted_iota(jnp.int32, (n, n), 1)
    ).astype(jnp.float32)
    near = 8 * (BAND + 1)
    trail, far = block[:near], block[near:]
    unit, far_unit = eye[:near], eye[near:]
    done = []
    head = [lane(trail[:8], j) for j in range(8)]
    for k in range(steps):
        if hooks and k in hooks:
            hooks[k]()
        c0 = 8 * k
        t_head, t_tail = trail[:8], trail[8:]
        u_head, u_tail = unit[:8], unit[8:]
        last = k == steps - 1
        if k % BAND == 0:
            band_rows, band_unit = [], []
        if not last:
            tail = [lane(t_tail, c0 + j) for j in range(8)]
            ahead = [lane(t_tail[:8], c0 + 8 + j) for j in range(8)]
        pivots = None
        for j in range(8):
            pivot = row(head[j], j)
            inv = 1.0 / pivot
            head_inv = head[j] * inv
            for q in range(j + 1, 8):
                m = row(head[q], j) * inv if q == j + 1 else row(head_inv, q)
                head[q] = head[q] - head[j] * m
                if not last:
                    tail[q] = tail[q] - scaled(tail[j], m)
            below = jnp.where(sublane > j, head[j], 0.0)
            u_row = row(u_head, j) * inv
            u_head = u_head - below * u_row
            if not last:
                first = tail[j][:8]
                first_inv = first * inv
                for q in range(8):
                    ahead[q] = ahead[q] - first * row(first_inv, q)
                t_row = row(t_head, j) * inv
                t_head = t_head - below * t_row
                t_tail = t_tail - scaled(tail[j], t_row)
                u_tail = u_tail - scaled(tail[j], u_row)
            pivots = pivot if pivots is None else jnp.where(sublane == j, pivot, pivots)
        scale = lax.rsqrt(pivots)
        done.append(u_head * scale)
        if last:
            break
        band_rows.append(t_head * scale)
        band_unit.append(done[-1])
        trail, unit, head = t_tail, u_tail, ahead
        if k % BAND == BAND - 1 and far is not None:
            top = n - far.shape[0]
            rows_done = jnp.concatenate(band_rows, axis=0)
            both = jnp.concatenate([rows_done, jnp.concatenate(band_unit, axis=0)], axis=1)
            change = stacked(rows_done, both, 0, 0)[top:]
            far, far_unit = far - change[:, :n], far_unit - change[:, n:]
            take = min(8 * BAND, n - top)
            trail = jnp.concatenate([trail, far[:take]], axis=0)
            unit = jnp.concatenate([unit, far_unit[:take]], axis=0)
            far, far_unit = (far[take:], far_unit[take:]) if top + take < n else (None, None)
    return jnp.concatenate(done, axis=0)


def kernel(
    maps_low, maps_high, leaf, out_low, out_high,
    slab, slab_in, front, p1_stage, p1, p2, lead, root, root_in, panel, c1, c2, q2, child, high, inv_high, left, pending, result,
    low_table, high_table, table_sems, load_sems, pair_sems,
    p1_cut, p2_cut, lead_cut, gather_send, gather_recv, piece_recv, stage_recv, p2_pair, out_sems,
    root_sems, c1_send, c1_recv, c2_sems, q2_sems, child_send, child_recv, high_sems,
):
    cube = lax.axis_index("cube")
    sub = lax.axis_index("sub")
    node = cube // 2
    core = cube % 2
    upper = node % 2
    other = node + 1 - 2 * upper
    partner = (cube + 1 - 2 * core, sub)
    across = (2 * other + core, sub)
    diagonal = (2 * other + 1 - core, sub)
    parts = ((SEP, HALF), (SEP + HALF, HALF), (0, SEP))

    def remote(src, dst, send_sem, recv_sem, device):
        return pltpu.make_async_remote_copy(
            src_ref=src, dst_ref=dst, send_sem=send_sem, recv_sem=recv_sem, device_id=device, device_id_type=MESH
        )

    def rows(i, base=0):
        return pl.ds(pl.multiple_of(base + 8 * i, 8), 8)

    def each_peer(fn):
        def step(t, carry):
            fn((sub + t) % BLOCKS)
            return carry

        lax.fori_loop(1, BLOCKS, step, 0)

    loads = [
        pltpu.make_async_copy(leaf.at[0, :, pl.ds(*part)], slab.at[:, pl.ds(*part)], load_sems.at[i])
        for i, part in enumerate(parts)
    ]
    tables = [
        pltpu.make_async_copy(maps_low, low_table, table_sems.at[0]),
        pltpu.make_async_copy(maps_high, high_table, table_sems.at[1]),
    ]
    for copy in loads + tables:
        copy.start()

    barrier = pltpu.get_barrier_semaphore()

    def greet(device):
        pl.semaphore_signal(barrier, inc=1, device_id=device, device_id_type=MESH)

    for device in (partner, across, diagonal):
        greet(device)
    each_peer(lambda i: greet((cube, i)))
    pl.when(sub != 1)(lambda: greet((partner[0], 1)))
    pl.when(sub != 1)(lambda: pl.semaphore_wait(barrier, BLOCKS + 2))
    pl.when(sub == 1)(lambda: pl.semaphore_wait(barrier, 2 * BLOCKS + 1))

    def p1_piece(cube_to, i):
        return remote(slab.at[rows(i), pl.ds(SEP, HALF)], p1_stage.at[core], p1_cut, stage_recv.at[core], (cube_to, i))

    loads[0].wait()

    @pl.when(sub == 1)
    def _():
        each_peer(lambda i: p1_piece(cube, i).start())
        each_peer(lambda i: p1_piece(partner[0], i).start())
        p1_piece(partner[0], sub).start()
        p1_stage[core] = slab[rows(sub), SEP : SEP + HALF]


    pairs = [
        remote(slab.at[:, pl.ds(*part)], slab_in.at[:, pl.ds(*part)], pair_sems.at[0, i], pair_sems.at[1, i], partner)
        for i, part in enumerate(parts)
    ]
    pairs[0].start()
    for load, copy in zip(loads[1:], pairs[1:]):
        load.wait()
        copy.start()
    for copy in tables:
        copy.wait()

    def tiles(block, table, index):
        moved = jnp.full((HALF, block.shape[1]), table[index, 2 * sub], jnp.int32) != 2 * sub
        first, second = block[:HALF, :], block[HALF:, :]
        return jnp.where(moved, second, first), jnp.where(moved, first, second)

    def extend_add(i):
        pairs[i].wait_recv()
        cols = slice(parts[i][0], sum(parts[i]))
        own = tiles(slab[:, cols], low_table, cube)
        theirs = tiles(slab_in[:, cols], low_table, cube + 1 - 2 * core)
        front[:HALF, cols] = own[0] + theirs[0]
        front[HALF:, cols] = own[1] + theirs[1]

    p2_columns = pl.ds(pl.multiple_of(SEP + core * HALF, HALF), HALF)

    def p2_piece(i):
        return remote(front.at[rows(i, HALF), p2_columns], p2.at[core, rows(i)], p2_cut.at[i], piece_recv.at[1], (cube, i))

    def lead_piece(i):
        return remote(front.at[rows(i, core * HALF)], lead.at[rows(i)], lead_cut.at[i], piece_recv.at[2], (cube, i))

    blocks = (p1, p2.at[core], lead)

    def share(n, i):
        own = blocks[n].at[rows(sub)]
        return remote(own, own, gather_send.at[n], gather_recv.at[n], (cube, i))

    def pass_on(n, owner):
        own = blocks[n].at[rows(sub)]

        @pl.when(sub != owner)
        def _():
            remote(own, own, gather_send.at[n], piece_recv.at[n], (cube, owner)).wait_recv()

        each_peer(lambda i: share(n, i).start())

    def all_shares(n):
        others = blocks[n].at[pl.ds(0, 8 * (BLOCKS - 1))]
        return remote(others, others, gather_send.at[n], gather_recv.at[n], partner)

    extend_add(0)
    extend_add(1)

    @pl.when(sub == 1)
    def _():
        each_peer(lambda i: p2_piece(i).start())
        p2[core, rows(sub), :] = front[rows(sub, HALF), p2_columns]

    extend_add(2)

    @pl.when(sub == 0)
    def _():
        each_peer(lambda i: lead_piece(i).start())
        lead[rows(sub), :] = front[rows(sub, core * HALF), :]

    for c in range(2):
        @pl.when(jnp.logical_or(sub != 1, core != c))
        def _():
            remote(p1_stage.at[c], p1_stage.at[c], p1_cut, stage_recv.at[c], partner).wait_recv()

    p1[rows(sub), :] = p1_stage[0] + p1_stage[1]
    each_peer(lambda i: share(0, i).start())
    pass_on(1, 1)
    pass_on(2, 0)

    all_shares(0).wait_recv()
    p2_copy = remote(p2.at[core], p2.at[core], p2_pair.at[0], p2_pair.at[1], partner)

    def p2_half():
        all_shares(1).wait_recv()
        p2_copy.start()

    inv1 = inverse_factor(p1[...], {P2_STEP: p2_half})
    p2_other = p2.at[1 - core]
    remote(p2_other, p2_other, p2_pair.at[0], p2_pair.at[1], partner).wait_recv()
    low = nt(p2[0], inv1)
    root_copies = [
        remote(root.at[:, part], root_in.at[:, part], root_sems.at[0, i], root_sems.at[1, i], partner)
        for i, part in enumerate((pl.ds(0, HALF), pl.ds(HALF, HALF)))
    ]

    def first_root():
        all_shares(2).wait_recv()
        root1 = nt(lead[:, SEP : SEP + HALF], inv1)
        root[:, :HALF] = root1
        pl.when(core == 0)(root_copies[0].start)
        left[0] = lead[:, SEP + HALF :] - nt(root1, low)
        left[1] = lead[:, pl.ds(pl.multiple_of(core * HALF, HALF), HALF)] - nt(root1, root1)

        child[core] = own_columns - nt(panel[0], root1)

    own_columns = front[:, pl.ds(pl.multiple_of(core * HALF, HALF), HALF)]

    def first_panel():
        panel[0] = nt(front[:, SEP : SEP + HALF], inv1)
        panel[1] = front[:, SEP + HALF :] - nt(panel[0], low)

    inv2 = inverse_factor(p2[1] - nt(low, low), {ROWS_STEP: first_panel, LEAD_STEP: first_root})
    root2 = nt(left[0], inv2)
    root[:, HALF:] = root2
    c1_copies = [
        remote(c1.at[0], c1.at[slot], c1_send.at[i], c1_recv.at[slot], device)
        for i, (slot, device) in enumerate(((0, partner), (1, across), (1, diagonal)))
    ]
    c2_copies = [
        remote(c2.at[0, part], c2.at[1, part], c2_sems.at[0, part], c2_sems.at[1, part], across) for part in range(2)
    ]

    @pl.when(core == 0)
    def _():
        root_copies[1].start()
        c1[0] = left[1] - nt(root2, root2)
        for copy in reversed(c1_copies):
            copy.start()

    @pl.when(core == 1)
    def _():
        c2[0, 1] = left[1] - nt(root2, root2)
        pl.when(upper == 0)(c2_copies[1].start)
        root_copies[0].wait_recv()
        across1 = nt(root[:, :HALF], root_in[:, :HALF])
        root_copies[1].wait_recv()
        c2[0, 0] = lead[:, :HALF] - across1 - nt(root2, root_in[:, HALF:])
        pl.when(upper == 0)(c2_copies[0].start)

    keep = (sub != 1).astype(jnp.float32)
    w2 = nt(panel[1], inv2)
    panel[1] = w2
    child[core] = (child[core] - nt(w2, root2)) * keep
    mine, theirs = child.at[core], child.at[2 + core]
    child_copies = [
        (remote(mine, theirs, child_send.at[0], child_recv.at[2 + core], across), jnp.logical_or(core == 0, upper == 0)),
        (remote(mine, mine, child_send.at[1], child_recv.at[core], partner), jnp.logical_and(core == 0, upper == 0)),
        (remote(mine, theirs, child_send.at[2], child_recv.at[2 + core], diagonal), jnp.logical_and(core == 0, upper == 1)),
    ]
    for copy, wanted in child_copies:
        pl.when(wanted)(copy.start)
    out_copies = [
        pltpu.make_async_copy(panel.at[core], out_low.at[0], out_sems.at[0]),
        pltpu.make_async_copy(result, out_high, out_sems.at[1]),
    ]
    out_copies[0].start()

    pl.when(core == 1)(c1_copies[0].wait_recv)
    c1_copies[1].wait_recv()
    high1 = inverse_factor(c1[0] + c1[1])
    inv_high[...] = high1
    share_rows = pl.ds(pl.multiple_of(core * 64, 64), 64)

    def child_wait(slot):
        remote(child.at[slot], child.at[slot], child_send.at[0], child_recv.at[slot], partner).wait_recv()

    def high_columns(half):
        own = tiles(child[half], high_table, node)
        theirs = tiles(child[2 + half], high_table, other)
        return jnp.concatenate([own[0] + theirs[0], own[1] + theirs[1]], axis=0)

    q2_copies = [remote(q2.at[part], q2.at[part], q2_sems.at[0, part], q2_sems.at[1, part], partner) for part in range(2)]
    high_copy = remote(high.at[core], high.at[core], high_sems.at[0], high_sems.at[1], partner)

    @pl.when(upper == 0)
    def _():
        pl.when(core == 1)(lambda: child_wait(0))
        child_wait(2)
        result[...] = nt(inv_high[share_rows, :], high_columns(0))

    @pl.when(upper == 1)
    def _():
        @pl.when(core == 1)
        def _():
            for part in (1, 0):
                c2_copies[part].wait_recv()
                q2[part] = c2[0, part] + c2[1, part]
                q2_copies[part].start()

        @pl.when(core == 0)
        def _():
            for part in (1, 0):
                q2_copies[part].wait_recv()

        high_low = nt(q2[0], high1)

        def own_high():
            child_wait(2 + core)
            high[core] = high_columns(core)
            high_copy.start()

        carried = dot(high_low, high1)
        other_half = high.at[1 - core]

        def both_high():
            remote(other_half, other_half, high_sems.at[0], high_sems.at[1], partner).wait_recv()
            pending[...] = high[1] - nt(high[0], carried)

        high2 = inverse_factor(q2[1] - nt(high_low, high_low), {OWN_STEP: own_high, BOTH_STEP: both_high})
        inv_high[...] = high2
        result[...] = nt(inv_high[share_rows, :], pending[...])

    out_copies[1].start()

    for copy in (*pairs, p2_copy):
        copy.wait_send()
    for n in range(3):
        all_shares(n).wait_send()

    @pl.when(sub == 1)
    def _():
        sent = slab_in.at[pl.ds(0, 8 * (2 * BLOCKS - 1)), pl.ds(0, HALF)]
        remote(sent, sent, p1_cut, stage_recv.at[0], partner).wait_send()
        each_peer(lambda i: p2_piece(i).wait_send())

    @pl.when(sub == 0)
    def _():
        each_peer(lambda i: lead_piece(i).wait_send())

    @pl.when(core == 0)
    def _():
        for copy in root_copies:
            copy.wait_send()
        for copy in c1_copies:
            copy.wait_send()

    @pl.when(core == 1)
    def _():
        for part in range(2):
            pl.when(upper == 0)(c2_copies[part].wait_send)
            pl.when(upper == 1)(q2_copies[part].wait_send)

    pl.when(upper == 1)(high_copy.wait_send)
    for copy, wanted in child_copies:
        pl.when(wanted)(copy.wait_send)
    for copy in out_copies:
        copy.wait()


def place(low, high, out_low, out_high):
    out_low[...] = low[...]
    out_high[...] = high[...]


def body(leaf_update, maps_low, maps_high):
    dma = pltpu.SemaphoreType.DMA

    def vmem(*shape):
        return pltpu.VMEM(shape, jnp.float32)

    low, high = pl.pallas_call(
        kernel,
        out_shape=(
            jax.ShapeDtypeStruct((1, SEP, HALF), jnp.float32),
            jax.ShapeDtypeStruct((HALF // 2, SEP), jnp.float32),
        ),
        in_specs=[pl.BlockSpec(memory_space=pl.ANY)] * 3,
        out_specs=(pl.BlockSpec(memory_space=pl.ANY),) * 2,
        scratch_shapes=[
            vmem(SEP, 2 * SEP), vmem(SEP, 2 * SEP), vmem(SEP, 2 * SEP),
            vmem(2, 8, HALF), vmem(HALF, HALF), vmem(2, HALF, HALF), vmem(HALF, 2 * SEP),
            vmem(HALF, SEP), vmem(HALF, SEP), vmem(2, SEP, HALF),
            vmem(2, HALF, HALF), vmem(2, 2, HALF, HALF), vmem(2, HALF, HALF), vmem(4, SEP, HALF), vmem(2, SEP, HALF),
            vmem(HALF, HALF), vmem(2, HALF, HALF), vmem(SEP, HALF), vmem(HALF // 2, SEP),
            pltpu.SMEM((32, 32), jnp.int32), pltpu.SMEM((16, 32), jnp.int32), dma((2,)), dma((3,)), dma((2, 3)),
            dma, dma((BLOCKS,)), dma((BLOCKS,)), dma((3,)), dma((3,)), dma((3,)), dma((2,)), dma((2,)), dma((2,)),
            dma((2, 2)), dma((3,)), dma((2,)), dma((2, 2)), dma((2, 2)), dma((3,)), dma((4,)), dma((2,)),
        ],
        compiler_params=pltpu.CompilerParams(
            collective_id=0, has_side_effects=True, vmem_limit_bytes=64 * 1024 * 1024
        ),
        cost_estimate=pl.CostEstimate(flops=2_000_000_000, bytes_accessed=1_000_000, transcendentals=0),
    )(maps_low, maps_high, leaf_update)
    low, high = pl.pallas_call(
        place,
        out_shape=(jax.ShapeDtypeStruct(low.shape, low.dtype), jax.ShapeDtypeStruct(high.shape, high.dtype)),
        in_specs=[pl.BlockSpec(memory_space=pltpu.VMEM)] * 2,
        out_specs=(pl.BlockSpec(memory_space=pltpu.VMEM),) * 2,
    )(low, high)
    return low, high.T[None]


def solution(mesh):
    in_specs = (P("cube", "sub", None), P(), P())
    out_specs = (P("cube", "sub", None), P("cube", "sub", None))
    return jax.shard_map(body, mesh=mesh, in_specs=in_specs, out_specs=out_specs, check_vma=False)
```
